128 devices in a mesh: ep: 32 (over x, y, core), ex: 4 (over z).
Axes of the slice: x: 4, y: 4, z: 4, core: 2. Of those that a mesh axis runs over, the one named last changes fastest.
Arguments:
- latent: bfloat16 [16384, 1024], P(('ep', 'ex')), may hold values from -6 to 6
- picks: int32 [16384, 4], P(('ep', 'ex')), may hold values from 0 to 63, all different within a row; in each aligned block of 128 rows (0 to 127, 128 to 255, ...) at most 10 rows name the same one
- gates: float32 [16384, 4], P(('ep', 'ex')), may hold values from 0.1 to 1
- gate_w: bfloat16 [128, 1024, 1024], P(('ep', 'ex')), may hold values from -0.1875 to 0.1875
- up_w: bfloat16 [128, 1024, 1024], P(('ep', 'ex')), may hold values from -0.1875 to 0.1875
- down_w: bfloat16 [128, 1024, 1024], P(('ep', 'ex')), may hold values from -0.125 to 0.125
- cotangent: bfloat16 [16384, 1024], P(('ep', 'ex')), may hold values from -6 to 6
Outputs:
- moe_out: bfloat16 [16384, 1024], P(('ep', 'ex'))
- d_latent: bfloat16 [16384, 1024], P(('ep', 'ex'))
- gate_grad: float32 [16384, 4], P(('ep', 'ex'))
- grad_gate_w: bfloat16 [128, 1024, 1024], P(('ep', 'ex'))
- grad_up_w: bfloat16 [128, 1024, 1024], P(('ep', 'ex'))
- grad_down_w: bfloat16 [128, 1024, 1024], P(('ep', 'ex'))
The draws below stay inside these ranges and needn't reach their ends.
Inputs may be any that keep to these rules, and one draw needn't show every extreme that they name: Each token names 4 different experts. Within the rows of one device no expert is named by more than 10 picks, a bound that some block reaches.
All inputs are finite; a program needn't handle non-finite values.
Results may differ from the reference program's by a relative error of at most 0.0065.
Values may be sent and summed in bfloat16 or wider, within the bound.
No kernel may reach another device: no remote copies, remote signals or barrier semaphores. Data moves between devices by JAX's collectives and lax.ppermute only.
A program may use at most 128 MiB of HBM per device.

```python
import math
import jax
import jax.numpy as jnp
import numpy as np
from jax import lax

L = 1024
FF = 2048
TOPK = 4
TOK_DEV = 128
EXPERTS = 64
CAP = 10
TOKENS = 16384
N_EP = 32
N_EX = 4


def steps_of(own_key, dims, shards, low, top_value):
    gain, own = 1.0, jax.random.fold_in(own_key, 6)
    for position, shards_of in shards:
        draws = jnp.exp(jax.random.uniform(jax.random.fold_in(own, position), (shards_of,), jnp.float32, low / len(shards), top_value / len(shards)))
        gain = gain * jnp.repeat(draws, dims[position] // shards_of).reshape([-1 if axis == position else 1 for axis in range(len(dims))])
    return gain


def shared_out(key, own, number, rows, number_of, top, bound, skew):
    order = jax.random.permutation(key, number_of)
    packed, usual = load_shares(number_of, rows * top, bound, skew, True), load_shares(number_of, rows * top, bound, skew, False)
    places = jnp.arange(number_of)

    def named(lengths, turn):
        used = int((lengths > 0).sum())
        fixed = max(1, used // 4)
        moved = fixed + (places - fixed + turn * (used - fixed)) % max(1, number_of - fixed)
        return jnp.zeros((number_of,), jnp.int32).at[order[jnp.where(places < fixed, places, moved)]].set(jnp.asarray(lengths, jnp.int32))

    lengths = jnp.where(number % 4 == 0, named(packed, number // 4), named(usual, number - number // 4 - 1))
    mixed = jax.random.permutation(jax.random.fold_in(own, 3), number_of)
    donor, sink = mixed[0:number_of // 2 * 2:2], mixed[1:number_of // 2 * 2:2]
    slack = jnp.minimum(lengths[donor] - 1, bound - lengths[sink]) // 2
    slack = jnp.where((donor == order[0]) | (sink == order[0]) | (lengths[sink] == 0), 0, jnp.maximum(slack, 0))
    moved = jax.random.randint(jax.random.fold_in(own, 4), (number_of // 2,), 0, 1 << 20) % (slack + 1)
    lengths = lengths.at[donor].add(-moved).at[sink].add(moved)
    members = jnp.searchsorted(jnp.cumsum(lengths), jnp.arange(rows * top), side="right").astype(jnp.int32)
    grid = members.reshape(top, rows).T
    grid = grid[jax.random.permutation(jax.random.fold_in(own, 1), rows)]
    turn = jax.random.randint(jax.random.fold_in(own, 2), (rows, 1), 0, top)
    return jnp.take_along_axis(grid, (jnp.arange(top)[None, :] + turn) % top, axis=1)


def load_shares(amount, total, bound, skew, full):
    weights = [(1 << 20) // math.isqrt(rank ** skew) + 1 for rank in range(1, amount + 1)]
    largest = bound if full else min(bound, max(-(-total // amount), total * weights[0] // sum(weights)))
    least = 1 if total - largest >= amount - 1 else 0
    holding, surplus = [largest] + [least] * (amount - 1), total - largest - least * (amount - 1)
    while surplus > 0:
        candidates = [i for i in range(1, amount) if holding[i] < largest] or [i for i in range(1, amount) if holding[i] < bound]
        pool, remaining = sum([weights[i] for i in candidates]), surplus
        for i in candidates:
            extra = min(bound - holding[i], max(1, remaining * weights[i] // pool), surplus)
            holding[i] = holding[i] + extra
            surplus = surplus - extra
    return np.array(holding)


def noise(rng, dims, scale, bound, split=(), held_as=jnp.bfloat16):
    drawn = scale * jax.random.normal(rng, dims, jnp.float32)
    if split:
        drawn = drawn * steps_of(rng, dims, split, -0.22, 0.18)
    return jnp.clip(drawn, -bound, bound).astype(held_as)


def setup_inputs(seed: int = 0) -> dict:
    keys = jax.random.split(jax.random.key(seed), 8)
    latent = noise(keys[0], (TOKENS, L), 1.0, 6.0, ((0, 128),))
    picks_keys = jax.random.split(jax.random.fold_in(keys[1], 1), TOKENS // TOK_DEV)
    picks_turns = jax.random.permutation(jax.random.fold_in(keys[1], 3), TOKENS // TOK_DEV)
    picks = jax.vmap(lambda own, number: shared_out(jax.random.fold_in(keys[1], 2), own, number, TOK_DEV, EXPERTS, TOPK, CAP, 2))(picks_keys, picks_turns).reshape((TOKENS, TOPK))
    gates = jnp.clip(0.1 + 0.9 * jax.random.uniform(keys[2], (TOKENS, TOPK), jnp.float32) ** steps_of(keys[2], (TOKENS, TOPK), ((0, 128),), -0.2, 0.2), 0.1, 1.0)
    gate_w = noise(keys[3], (2 * EXPERTS, L, FF // 2), L ** -0.5, 0.1875, ((0, 128),))
    up_w = noise(keys[4], (2 * EXPERTS, L, FF // 2), L ** -0.5, 0.1875, ((0, 128),))
    down_w = noise(keys[5], (2 * EXPERTS, FF // 2, L), FF ** -0.5, 0.125, ((0, 128),))
    cotangent = noise(keys[6], (TOKENS, L), 1.0, 6.0, ((0, 128),))
    return dict(latent=latent, picks=picks, gates=gates, gate_w=gate_w, up_w=up_w, down_w=down_w, cotangent=cotangent)


def slots_of(pick_rows, count_experts):
    flat_ids = pick_rows.reshape(-1)
    onehot = (flat_ids[:, None] == jnp.arange(count_experts, dtype=jnp.int32)[None, :]).astype(jnp.int32)
    before = jnp.cumsum(onehot, axis=0) - onehot
    return jnp.sum(before * onehot, axis=1).reshape(pick_rows.shape).astype(jnp.int32)


def silu_parts(pre_gate):
    sigma = jax.nn.sigmoid(pre_gate)
    return pre_gate * sigma, sigma * (1.0 + pre_gate * (1.0 - sigma))


def reference(latent, picks, gates, gate_w, up_w, down_w, cotangent):
    devices = N_EP * N_EX
    half_ff = FF // 2
    full_gate = gate_w.reshape(EXPERTS, 2, L, half_ff).transpose(0, 2, 1, 3).reshape(EXPERTS, L, FF)
    full_up = up_w.reshape(EXPERTS, 2, L, half_ff).transpose(0, 2, 1, 3).reshape(EXPERTS, L, FF)
    full_down = down_w.reshape(EXPERTS, FF, L)
    picks_dev = picks.reshape(devices, TOK_DEV, TOPK)
    slot_ids = jax.vmap(lambda rows: slots_of(rows, EXPERTS))(picks_dev)
    target = (picks_dev * CAP + slot_ids).astype(jnp.int32)
    gates_dev = gates.reshape(devices, TOK_DEV, TOPK)
    cot_dev = cotangent.reshape(devices, TOK_DEV, L)

    def build(values, target_one):
        return jnp.zeros((EXPERTS * CAP, L), jnp.bfloat16).at[target_one.reshape(-1)].set(values.reshape(-1, L))

    def to_experts(sent):
        return sent.reshape(devices, EXPERTS, CAP, L).transpose(1, 0, 2, 3).reshape(EXPERTS, devices * CAP, L)

    def to_sources(done):
        return done.reshape(EXPERTS, devices, CAP, L).transpose(1, 0, 2, 3).reshape(devices, EXPERTS * CAP, L)

    spread = jnp.broadcast_to(latent.reshape(devices, TOK_DEV, 1, L), (devices, TOK_DEV, TOPK, L))
    arrived = to_experts(jax.vmap(build)(spread, target))

    def forward(operands):
        rows, w_gate, w_up, w_down = operands
        pre_gate = jnp.dot(rows, w_gate, preferred_element_type=jnp.float32)
        pre_up = jnp.dot(rows, w_up, preferred_element_type=jnp.float32)
        active, slope = silu_parts(pre_gate)
        hidden = (active * pre_up).astype(jnp.bfloat16)
        return jnp.dot(hidden, w_down, preferred_element_type=jnp.float32).astype(jnp.bfloat16)

    expert_out = lax.map(forward, (arrived, full_gate, full_up, full_down))
    back = to_sources(expert_out)
    picked = jax.vmap(lambda buf, idx: buf[idx])(back, target).astype(jnp.float32)
    moe_out = jnp.sum(gates_dev[..., None] * picked, axis=2).astype(jnp.bfloat16).reshape(TOKENS, L)
    gate_grad = jnp.sum(cot_dev[:, :, None, :].astype(jnp.float32) * picked, axis=-1).reshape(TOKENS, TOPK)

    weighted = (gates_dev[..., None] * cot_dev[:, :, None, :].astype(jnp.float32)).astype(jnp.bfloat16)
    d_arrived = to_experts(jax.vmap(build)(weighted, target))

    def backward(operands):
        rows, d_out, w_gate, w_up, w_down = operands
        pre_gate = jnp.dot(rows, w_gate, preferred_element_type=jnp.float32)
        pre_up = jnp.dot(rows, w_up, preferred_element_type=jnp.float32)
        active, slope = silu_parts(pre_gate)
        hidden = (active * pre_up).astype(jnp.bfloat16)
        d_hidden = jnp.dot(d_out, w_down.T, preferred_element_type=jnp.float32)
        grad_down = jnp.dot(hidden.T, d_out, preferred_element_type=jnp.float32).astype(jnp.bfloat16)
        d_pre_gate = (d_hidden * pre_up * slope).astype(jnp.bfloat16)
        d_pre_up = (d_hidden * active).astype(jnp.bfloat16)
        grad_gate = jnp.dot(rows.T, d_pre_gate, preferred_element_type=jnp.float32).astype(jnp.bfloat16)
        grad_up = jnp.dot(rows.T, d_pre_up, preferred_element_type=jnp.float32).astype(jnp.bfloat16)
        d_rows = (jnp.dot(d_pre_gate, w_gate.T, preferred_element_type=jnp.float32)
                  + jnp.dot(d_pre_up, w_up.T, preferred_element_type=jnp.float32)).astype(jnp.bfloat16)
        return d_rows, grad_gate, grad_up, grad_down

    d_rows, grad_gate_full, grad_up_full, grad_down_full = lax.map(backward, (arrived, d_arrived, full_gate, full_up, full_down))
    d_back = to_sources(d_rows)
    d_picked = jax.vmap(lambda buf, idx: buf[idx])(d_back, target).astype(jnp.float32)
    d_latent = jnp.sum(d_picked, axis=2).astype(jnp.bfloat16).reshape(TOKENS, L)
    grad_gate_w = grad_gate_full.reshape(EXPERTS, L, 2, half_ff).transpose(0, 2, 1, 3).reshape(2 * EXPERTS, L, half_ff)
    grad_up_w = grad_up_full.reshape(EXPERTS, L, 2, half_ff).transpose(0, 2, 1, 3).reshape(2 * EXPERTS, L, half_ff)
    grad_down_w = grad_down_full.reshape(2 * EXPERTS, half_ff, L)
    return moe_out, d_latent, gate_grad, grad_gate_w, grad_up_w, grad_down_w
```

```python
import functools

import jax
import jax.numpy as jnp
import numpy as np
from jax import lax
from jax.experimental import pallas as pl
from jax.experimental.pallas import tpu as pltpu
from jax.sharding import PartitionSpec as P

BF16 = jnp.bfloat16
F32 = jnp.float32
AXES = ("ep", "ex")
TOPK = 4
CAP = 10
PIECES = 4
GROUP = 8
VMEM_LIMIT = 48 * 1024 * 1024
STEPS = 4


def dot(a, b, ca=1, cb=0):
    return lax.dot_general(a, b, (((ca,), (cb,)), ((), ())), preferred_element_type=F32)


def one_hot(mask):
    return jnp.where(mask, 1.0, 0.0).astype(BF16)


def returned_codes(experts):
    slots = np.arange(experts * CAP, dtype=np.int32).reshape(experts, 1, CAP)
    return np.broadcast_to(slots, (experts, 2, CAP)).reshape(STEPS, 1, experts * 2 * CAP // STEPS)


def unpack_table():
    size = GROUP * PIECES * CAP
    table = np.zeros((size, size), np.float32)
    for block in range(GROUP):
        for piece in range(PIECES):
            for slot in range(CAP):
                table[(piece * GROUP + block) * CAP + slot, (block * PIECES + piece) * CAP + slot] = 1
    return table


def double_table():
    table = unpack_table().T.reshape(GROUP, 1, PIECES * CAP, -1)
    return np.broadcast_to(table, (GROUP, 2) + table.shape[2:]).reshape(-1, table.shape[-1])


def call(kernel, grid, in_specs, out_specs, out_shape, scratch=(), flops=0, moved=0):
    return pl.pallas_call(
        kernel,
        grid=grid,
        in_specs=in_specs,
        out_specs=out_specs,
        out_shape=out_shape,
        scratch_shapes=list(scratch),
        compiler_params=pltpu.CompilerParams(vmem_limit_bytes=VMEM_LIMIT),
        cost_estimate=pl.CostEstimate(flops=flops, bytes_accessed=moved, transcendentals=0),
    )


def fixed(shape):
    return pl.BlockSpec(shape, lambda i: (0,) * len(shape))


def rows_of(count, width):
    return pl.BlockSpec((count, width), lambda i: (i, 0))


def pieces(rows):
    width = rows.shape[1] // PIECES
    return jnp.concatenate([rows[:, p * width : (p + 1) * width] for p in range(PIECES)], axis=0)


def send(rows, table, sent_ref):
    inner = GROUP * CAP
    size = table.shape[0]
    for group in range(rows.shape[0] // inner):
        part = dot(table[...], pieces(rows[group * inner : (group + 1) * inner, :]))
        sent_ref[group * size : (group + 1) * size, :] = part.astype(BF16)


def repack(rows, table, back_ref):
    inner = GROUP * CAP
    size = table.shape[0]
    for group in range(rows.shape[0] // inner):
        part = dot(table[...], pieces(rows[group * inner : (group + 1) * inner, :]))
        back_ref[group * size : (group + 1) * size, :] = part.astype(BF16)


def unpack(back_ref, table):
    size = table.shape[0]
    inner = GROUP * CAP
    groups = []
    for group in range(back_ref.shape[0] // size):
        mixed = dot(table[...], back_ref[group * size : (group + 1) * size, :]).astype(BF16)
        groups.append(jnp.concatenate([mixed[p * inner : (p + 1) * inner, :] for p in range(PIECES)], axis=1))
    return jnp.concatenate(groups, axis=0)


def route_kernel(picks_ref, latent_ref, table, target_ref, sent_ref):
    picks = picks_ref[...]
    tokens = picks.shape[0]
    lane = lax.broadcasted_iota(jnp.int32, (tokens, 128), 1)
    named = [picks[:, k : k + 1] == lane for k in range(TOPK)]
    some = functools.reduce(jnp.logical_or, named)
    now = lax.broadcasted_iota(jnp.int32, (tokens, tokens), 0)
    other = lax.broadcasted_iota(jnp.int32, (tokens, tokens), 1)
    before = dot(one_hot(other < now), one_hot(some))
    slots = sent_ref.shape[0] // (2 * PIECES)
    codes = lax.broadcasted_iota(jnp.int32, (1, slots), 1)
    hit = None
    for k in range(TOPK):
        slot = jnp.sum(jnp.where(named[k], before, 0.0), axis=1, keepdims=True)
        target = picks[:, k : k + 1] * CAP + slot.astype(jnp.int32)
        target_ref[:, k : k + 1] = target
        here = target == codes
        hit = here if hit is None else hit | here
    send(dot(one_hot(hit), latent_ref[...], 0, 0).astype(BF16), table, sent_ref)


def pack_kernel(target_ref, gates_ref, cotangent_ref, table, sent_ref):
    cotangent = cotangent_ref[...].astype(F32)
    weighted = jnp.concatenate([(gates_ref[:, k : k + 1] * cotangent).astype(BF16) for k in range(TOPK)], axis=0)
    slots = sent_ref.shape[0] // (2 * PIECES)
    codes = lax.broadcasted_iota(jnp.int32, (1, slots), 1)
    hits = jnp.concatenate([one_hot(target_ref[:, k : k + 1] == codes) for k in range(TOPK)], axis=0)
    send(dot(hits, weighted, 0, 0).astype(BF16), table, sent_ref)


def forward_kernel(moved_ref, w_gate, w_up, w_down, apart, together, rows_ref, active_ref, slope_ref, hidden_ref, back_ref):
    rows = unpack(moved_ref, apart)
    rows_ref[...] = rows
    pre_gate = dot(rows, w_gate[...])
    pre_up = dot(rows, w_up[...])
    sigma = jax.nn.sigmoid(pre_gate)
    active = pre_gate * sigma
    hidden = (active * pre_up).astype(BF16)
    active_ref[...] = active
    slope_ref[...] = pre_up * (sigma * (1.0 + pre_gate * (1.0 - sigma)))
    hidden_ref[...] = hidden
    repack(dot(hidden, w_down[...]).astype(BF16), together, back_ref)


def backward_kernel(moved_ref, active_ref, slope_ref, w_gate, w_up, w_down, apart, together, rows_ref, d_gate_ref, d_up_ref, back_ref):
    rows = unpack(moved_ref, apart)
    rows_ref[...] = rows
    d_hidden = dot(rows, w_down[...], 1, 1)
    d_gate = (d_hidden * slope_ref[...]).astype(BF16)
    d_up = (d_hidden * active_ref[...]).astype(BF16)
    d_gate_ref[...] = d_gate
    d_up_ref[...] = d_up
    d_rows = dot(d_gate, w_gate[...], 1, 1) + dot(d_up, w_up[...], 1, 1)
    repack(d_rows.astype(BF16), together, back_ref)


def moe_kernel(back_ref, codes_ref, target_ref, gates_ref, cotangent_ref, table, moe_ref, gate_grad_ref, picked):
    step = pl.program_id(0)
    tokens = target_ref.shape[0]
    codes = codes_ref[0]
    hits = jnp.concatenate([one_hot(target_ref[:, k : k + 1] == codes) for k in range(TOPK)], axis=0)
    part = dot(hits, unpack(back_ref, table))

    @pl.when(step == 0)
    def _():
        picked[...] = part

    @pl.when(step > 0)
    def _():
        picked[...] += part

    @pl.when(step == pl.num_programs(0) - 1)
    def _():
        cotangent = cotangent_ref[...].astype(F32)
        total = None
        for k in range(TOPK):
            mine = picked[k * tokens : (k + 1) * tokens, :]
            gate_grad_ref[:, k : k + 1] = jnp.sum(cotangent * mine, axis=1, keepdims=True)
            term = gates_ref[:, k : k + 1] * mine
            total = term if total is None else total + term
        moe_ref[...] = total.astype(BF16)


def latent_kernel(back_ref, codes_ref, target_ref, table, out_ref, total):
    step = pl.program_id(0)
    codes = codes_ref[0]
    hit = functools.reduce(jnp.logical_or, [target_ref[:, k : k + 1] == codes for k in range(TOPK)])
    part = dot(one_hot(hit), unpack(back_ref, table))

    @pl.when(step == 0)
    def _():
        total[...] = part

    @pl.when(step > 0)
    def _():
        total[...] += part

    @pl.when(step == pl.num_programs(0) - 1)
    def _():
        out_ref[...] = total[...].astype(BF16)


def exchange(blocks, devices):
    shape = blocks.shape
    blocks = blocks.reshape(devices, shape[0] // devices, shape[1])
    moved = lax.all_to_all(blocks, AXES, split_axis=0, concat_axis=0, tiled=True).reshape(shape)
    return pltpu.with_memory_space_constraint(moved, pltpu.HBM)


def shards(latent, picks, gates, gate_w, up_w, down_w, cotangent):
    tokens, width = latent.shape
    devices = lax.axis_size("ep") * lax.axis_size("ex")
    experts = devices // 2
    w_gate, w_up, w_down = gate_w[0], up_w[0], down_w[0]
    hidden_width = w_gate.shape[1]
    total_rows, back_rows = devices * CAP, devices * CAP * PIECES
    piece = width // PIECES
    back_shape = pltpu.HBM((back_rows, piece), BF16)
    apart, together, doubled = [jnp.asarray(t, BF16) for t in (unpack_table(), unpack_table().T, double_table())]
    codes = jnp.asarray(returned_codes(experts))

    target, sent = call(
        route_kernel,
        (1,),
        [fixed(picks.shape), fixed(latent.shape), fixed(doubled.shape)],
        [fixed(picks.shape), fixed(back_shape.shape)],
        [jax.ShapeDtypeStruct(picks.shape, jnp.int32), back_shape],
        flops=2 * total_rows * tokens * width,
        moved=2 * (total_rows + tokens) * width,
    )(picks, latent, doubled)
    moved = exchange(sent, devices)
    d_sent = call(
        pack_kernel,
        (1,),
        [fixed(picks.shape), fixed(gates.shape), fixed(cotangent.shape), fixed(doubled.shape)],
        fixed(back_shape.shape),
        back_shape,
        flops=2 * total_rows * tokens * TOPK * width,
        moved=2 * (total_rows + tokens) * width,
    )(target, gates, cotangent, doubled)
    d_moved = exchange(d_sent, devices)

    block = total_rows // STEPS
    weights = [fixed(w_gate.shape), fixed(w_up.shape), fixed(w_down.shape), fixed(apart.shape), fixed(apart.shape)]
    row_spec, hidden_spec = rows_of(block, width), rows_of(block, hidden_width)
    back_spec = rows_of(back_rows // STEPS, piece)
    row_shape = jax.ShapeDtypeStruct((total_rows, width), BF16)
    hidden_shape = jax.ShapeDtypeStruct((total_rows, hidden_width), BF16)
    wide_shape = jax.ShapeDtypeStruct((total_rows, hidden_width), F32)
    rows, active, slope, hidden, back = call(
        forward_kernel,
        (STEPS,),
        [back_spec] + weights,
        [row_spec, hidden_spec, hidden_spec, hidden_spec, back_spec],
        [row_shape, wide_shape, wide_shape, hidden_shape, back_shape],
        flops=6 * total_rows * width * hidden_width,
        moved=6 * width * hidden_width + 18 * total_rows * width,
    )(moved, w_gate, w_up, w_down, apart, together)
    returned = exchange(back, devices)
    d_rows, d_gate, d_up, d_back = call(
        backward_kernel,
        (STEPS,),
        [back_spec, hidden_spec, hidden_spec] + weights,
        [row_spec, hidden_spec, hidden_spec, back_spec],
        [row_shape, hidden_shape, hidden_shape, back_shape],
        flops=6 * total_rows * width * hidden_width,
        moved=6 * width * hidden_width + 18 * total_rows * width,
    )(d_moved, active, slope, w_gate, w_up, w_down, apart, together)
    d_returned = exchange(d_back, devices)

    grad_gate = jnp.dot(rows.T, d_gate, preferred_element_type=F32).astype(BF16)
    grad_up = jnp.dot(rows.T, d_up, preferred_element_type=F32).astype(BF16)
    grad_down = jnp.dot(hidden.T, d_rows, preferred_element_type=F32).astype(BF16)

    codes_spec = pl.BlockSpec((1,) + codes.shape[1:], lambda i: (i, 0, 0))
    moe_out, gate_grad = call(
        moe_kernel,
        (STEPS,),
        [back_spec, codes_spec, fixed(picks.shape), fixed(gates.shape), fixed(cotangent.shape), fixed(apart.shape)],
        [fixed(latent.shape), fixed(gates.shape)],
        [jax.ShapeDtypeStruct(latent.shape, BF16), jax.ShapeDtypeStruct(gates.shape, F32)],
        [pltpu.VMEM((TOPK * tokens, width), F32)],
        flops=2 * total_rows * tokens * TOPK * width,
        moved=2 * back_rows * piece,
    )(returned, codes, target, gates, cotangent, apart)
    d_latent = call(
        latent_kernel,
        (STEPS,),
        [back_spec, codes_spec, fixed(picks.shape), fixed(apart.shape)],
        fixed(latent.shape),
        jax.ShapeDtypeStruct(latent.shape, BF16),
        [pltpu.VMEM((tokens, width), F32)],
        flops=2 * total_rows * tokens * width,
        moved=2 * back_rows * piece,
    )(d_returned, codes, target, apart)
    return (moe_out, d_latent, gate_grad, grad_gate[None], grad_up[None], grad_down[None])


def solution(mesh):
    rows, blocks = P(AXES, None), P(AXES, None, None)
    return jax.shard_map(
        shards,
        mesh=mesh,
        in_specs=(rows, rows, rows, blocks, blocks, blocks, rows),
        out_specs=(rows, rows, rows, blocks, blocks, blocks),
        check_vma=False,
    )
```

```python
import functools

import jax
import jax.numpy as jnp
import numpy as np
from jax import lax
from jax.experimental import pallas as pl
from jax.experimental.pallas import tpu as pltpu
from jax.sharding import PartitionSpec as P

BF16 = jnp.bfloat16
F32 = jnp.float32
AXES = ("ep", "ex")
TOPK = 4
CAP = 10
PIECES = 4
GROUP = 8
VMEM_LIMIT = 48 * 1024 * 1024
STEPS = 4


def dot(a, b, ca=1, cb=0):
    return lax.dot_general(a, b, (((ca,), (cb,)), ((), ())), preferred_element_type=F32)


def one_hot(mask):
    return jnp.where(mask, 1.0, 0.0).astype(BF16)


def returned_codes(experts):
    slots = np.arange(experts * CAP, dtype=np.int32).reshape(experts, 1, CAP)
    return np.broadcast_to(slots, (experts, 2, CAP)).reshape(-1, 1)


def unpack_table():
    size = GROUP * PIECES * CAP
    table = np.zeros((size, size), np.float32)
    for block in range(GROUP):
        for piece in range(PIECES):
            for slot in range(CAP):
                table[(piece * GROUP + block) * CAP + slot, (block * PIECES + piece) * CAP + slot] = 1
    return table


def double_table():
    table = unpack_table().T.reshape(GROUP, 1, PIECES * CAP, -1)
    return np.broadcast_to(table, (GROUP, 2) + table.shape[2:]).reshape(-1, table.shape[-1])


def call(kernel, grid, in_specs, out_specs, out_shape, scratch=(), flops=0, moved=0):
    return pl.pallas_call(
        kernel,
        grid=grid,
        in_specs=in_specs,
        out_specs=out_specs,
        out_shape=out_shape,
        scratch_shapes=list(scratch),
        compiler_params=pltpu.CompilerParams(vmem_limit_bytes=VMEM_LIMIT),
        cost_estimate=pl.CostEstimate(flops=flops, bytes_accessed=moved, transcendentals=0),
    )


def fixed(shape):
    return pl.BlockSpec(shape, lambda i: (0,) * len(shape))


def rows_of(count, width):
    return pl.BlockSpec((count, width), lambda i: (i, 0))


def pieces(rows):
    width = rows.shape[1] // PIECES
    return jnp.concatenate([rows[:, p * width : (p + 1) * width] for p in range(PIECES)], axis=0)


def send(rows, table, sent_ref, ready, sems):
    inner = GROUP * CAP
    size = table.shape[0]
    copies = []
    for group in range(rows.shape[0] // inner):
        part = dot(table[...], pieces(rows[group * inner : (group + 1) * inner, :]))
        ready[group] = part.astype(BF16)
        place = sent_ref.at[group * size : (group + 1) * size, :]
        copies.append(pltpu.make_async_copy(ready.at[group], place, sems.at[group]))
        copies[-1].start()
    for copy in copies:
        copy.wait()


def repack(rows, table, back_ref):
    inner = GROUP * CAP
    size = table.shape[0]
    for group in range(rows.shape[0] // inner):
        part = dot(table[...], pieces(rows[group * inner : (group + 1) * inner, :]))
        back_ref[group * size : (group + 1) * size, :] = part.astype(BF16)


def unpack(back_ref, table):
    size = table.shape[0]
    inner = GROUP * CAP
    groups = []
    for group in range(back_ref.shape[0] // size):
        mixed = dot(table[...], back_ref[group * size : (group + 1) * size, :]).astype(BF16)
        groups.append(jnp.concatenate([mixed[p * inner : (p + 1) * inner, :] for p in range(PIECES)], axis=1))
    return jnp.concatenate(groups, axis=0)


def column(row):
    count = row.shape[1]
    here = lax.broadcasted_iota(jnp.int32, (count, count), 0) == lax.broadcasted_iota(jnp.int32, (count, count), 1)
    return jnp.sum(jnp.where(here, row, 0), axis=1, keepdims=True)


def row_of(values):
    count = values.shape[0]
    here = lax.broadcasted_iota(jnp.int32, (count, count), 0) == lax.broadcasted_iota(jnp.int32, (count, count), 1)
    return jnp.sum(jnp.where(here, values, 0), axis=0, keepdims=True)


def route_kernel(picks_ref, latent_ref, table, target_ref, sent_ref, ready, sems):
    picks = picks_ref[...]
    tokens = picks.shape[1]
    slots = sent_ref.shape[0] // (2 * PIECES)
    names = lax.broadcasted_iota(jnp.int32, (slots // CAP, tokens), 0)
    named = [picks[k : k + 1, :] == names for k in range(TOPK)]
    some = functools.reduce(jnp.logical_or, named)
    other = lax.broadcasted_iota(jnp.int32, (tokens, tokens), 0)
    now = lax.broadcasted_iota(jnp.int32, (tokens, tokens), 1)
    before = dot(one_hot(some), one_hot(other < now))
    codes = lax.broadcasted_iota(jnp.int32, (slots, tokens), 0)
    hit = None
    for k in range(TOPK):
        slot = jnp.sum(jnp.where(named[k], before, 0.0), axis=0, keepdims=True)
        target = picks[k : k + 1, :] * CAP + slot.astype(jnp.int32)
        target_ref[k : k + 1, :] = target
        here = codes == target
        hit = here if hit is None else hit | here
    rows = dot(one_hot(hit), latent_ref[...]).astype(BF16)
    send(rows, table, sent_ref, ready, sems)


def pack_kernel(target_ref, gates_ref, cotangent_ref, table, sent_ref, ready, sems):
    cotangent = cotangent_ref[...].astype(F32)
    tokens = cotangent.shape[0]
    slots = sent_ref.shape[0] // (2 * PIECES)
    codes = lax.broadcasted_iota(jnp.int32, (slots, tokens), 0)
    hits, weighted = [], []
    for k in range(TOPK):
        hits.append(one_hot(codes == target_ref[k : k + 1, :]))
        weighted.append((column(gates_ref[k : k + 1, :]) * cotangent).astype(BF16))
    rows = dot(jnp.concatenate(hits, axis=1), jnp.concatenate(weighted, axis=0)).astype(BF16)
    send(rows, table, sent_ref, ready, sems)


def forward_kernel(moved_ref, w_gate, w_up, w_down, apart, together, rows_ref, active_ref, slope_ref, hidden_ref, back_ref):
    rows = unpack(moved_ref, apart)
    rows_ref[...] = rows
    pre_gate = dot(rows, w_gate[...])
    pre_up = dot(rows, w_up[...])
    sigma = jax.nn.sigmoid(pre_gate)
    active = pre_gate * sigma
    hidden = (active * pre_up).astype(BF16)
    active_ref[...] = active
    slope_ref[...] = pre_up * (sigma * (1.0 + pre_gate * (1.0 - sigma)))
    hidden_ref[...] = hidden
    repack(dot(hidden, w_down[...]).astype(BF16), together, back_ref)


def backward_kernel(moved_ref, active_ref, slope_ref, w_gate, w_up, w_down, apart, together, rows_ref, d_gate_ref, d_up_ref, back_ref):
    rows = unpack(moved_ref, apart)
    rows_ref[...] = rows
    d_hidden = dot(rows, w_down[...], 1, 1)
    d_gate = (d_hidden * slope_ref[...]).astype(BF16)
    d_up = (d_hidden * active_ref[...]).astype(BF16)
    d_gate_ref[...] = d_gate
    d_up_ref[...] = d_up
    d_rows = dot(d_gate, w_gate[...], 1, 1) + dot(d_up, w_up[...], 1, 1)
    repack(d_rows.astype(BF16), together, back_ref)


def moe_kernel(back_ref, codes_ref, target_ref, gates_ref, cotangent_ref, table, moe_ref, gate_grad_ref, picked):
    step = pl.program_id(0)
    tokens = target_ref.shape[1]
    codes = codes_ref[...]
    hits = jnp.concatenate([one_hot(codes == target_ref[k : k + 1, :]) for k in range(TOPK)], axis=1)
    part = dot(hits, unpack(back_ref, table), 0, 0)

    @pl.when(step == 0)
    def _():
        picked[...] = part

    @pl.when(step > 0)
    def _():
        picked[...] += part

    @pl.when(step == pl.num_programs(0) - 1)
    def _():
        cotangent = cotangent_ref[...].astype(F32)
        total = None
        for k in range(TOPK):
            mine = picked[k * tokens : (k + 1) * tokens, :]
            gate_grad_ref[k : k + 1, :] = row_of(jnp.sum(cotangent * mine, axis=1, keepdims=True))
            term = column(gates_ref[k : k + 1, :]) * mine
            total = term if total is None else total + term
        moe_ref[...] = total.astype(BF16)


def latent_kernel(back_ref, codes_ref, target_ref, table, out_ref):
    codes = codes_ref[...]
    hit = functools.reduce(jnp.logical_or, [codes == target_ref[k : k + 1, :] for k in range(TOPK)])
    out_ref[...] = dot(one_hot(hit), unpack(back_ref, table), 0, 0).astype(BF16)


def exchange(blocks, devices):
    shape = blocks.shape
    blocks = blocks.reshape(devices, shape[0] // devices, shape[1])
    return lax.all_to_all(blocks, AXES, split_axis=0, concat_axis=0, tiled=True).reshape(shape)


def in_hbm(value):
    return pltpu.with_memory_space_constraint(value, pltpu.HBM)


def shards(latent, picks, gates, gate_w, up_w, down_w, cotangent):
    tokens, width = latent.shape
    devices = lax.axis_size("ep") * lax.axis_size("ex")
    experts = devices // 2
    w_gate, w_up, w_down = gate_w[0], up_w[0], down_w[0]
    hidden_width = w_gate.shape[1]
    total_rows, back_rows = devices * CAP, devices * CAP * PIECES
    piece = width // PIECES
    back_shape = pltpu.HBM((back_rows, piece), BF16)
    apart, together, doubled = [jnp.asarray(t, BF16) for t in (unpack_table(), unpack_table().T, double_table())]
    codes = jnp.asarray(returned_codes(experts))

    picks, gates = picks.T, gates.T
    groups = experts // GROUP
    sending = [pltpu.VMEM((groups, doubled.shape[0], piece), BF16), pltpu.SemaphoreType.DMA((groups,))]
    sent_spec = pl.BlockSpec(memory_space=pltpu.HBM)
    target, sent = call(
        route_kernel,
        (1,),
        [fixed(picks.shape), fixed(latent.shape), fixed(doubled.shape)],
        [fixed(picks.shape), sent_spec],
        [jax.ShapeDtypeStruct(picks.shape, jnp.int32), back_shape],
        sending,
        flops=2 * total_rows * tokens * width,
        moved=2 * (total_rows + tokens) * width,
    )(in_hbm(picks), in_hbm(latent), in_hbm(doubled))
    moved = in_hbm(exchange(sent, devices))
    d_sent = call(
        pack_kernel,
        (1,),
        [fixed(picks.shape), fixed(gates.shape), fixed(cotangent.shape), fixed(doubled.shape)],
        sent_spec,
        back_shape,
        sending,
        flops=2 * total_rows * tokens * TOPK * width,
        moved=2 * (total_rows + tokens) * width,
    )(target, gates, cotangent, doubled)
    d_moved = in_hbm(exchange(d_sent, devices))

    block = total_rows // STEPS
    weights = [fixed(w_gate.shape), fixed(w_up.shape), fixed(w_down.shape), fixed(apart.shape), fixed(apart.shape)]
    row_spec, hidden_spec = rows_of(block, width), rows_of(block, hidden_width)
    back_spec = rows_of(back_rows // STEPS, piece)
    row_shape = jax.ShapeDtypeStruct((total_rows, width), BF16)
    hidden_shape = jax.ShapeDtypeStruct((total_rows, hidden_width), BF16)
    wide_shape = jax.ShapeDtypeStruct((total_rows, hidden_width), F32)
    rows, active, slope, hidden, back = call(
        forward_kernel,
        (STEPS,),
        [back_spec] + weights,
        [row_spec, hidden_spec, hidden_spec, hidden_spec, back_spec],
        [row_shape, wide_shape, wide_shape, hidden_shape, back_shape],
        flops=6 * total_rows * width * hidden_width,
        moved=6 * width * hidden_width + 18 * total_rows * width,
    )(moved, w_gate, w_up, w_down, apart, together)
    returned = in_hbm(exchange(back, devices))
    d_rows, d_gate, d_up, d_back = call(
        backward_kernel,
        (STEPS,),
        [back_spec, hidden_spec, hidden_spec] + weights,
        [row_spec, hidden_spec, hidden_spec, back_spec],
        [row_shape, hidden_shape, hidden_shape, back_shape],
        flops=6 * total_rows * width * hidden_width,
        moved=6 * width * hidden_width + 18 * total_rows * width,
    )(d_moved, active, slope, w_gate, w_up, w_down, apart, together)
    d_returned = exchange(d_back, devices)

    grad_gate = jnp.dot(rows.T, d_gate, preferred_element_type=F32).astype(BF16)
    grad_up = jnp.dot(rows.T, d_up, preferred_element_type=F32).astype(BF16)
    grad_down = jnp.dot(hidden.T, d_rows, preferred_element_type=F32).astype(BF16)

    codes_spec = rows_of(total_rows // STEPS, 1)
    moe_out, gate_grad = call(
        moe_kernel,
        (STEPS,),
        [back_spec, codes_spec, fixed(picks.shape), fixed(gates.shape), fixed(cotangent.shape), fixed(apart.shape)],
        [fixed(latent.shape), fixed(gates.shape)],
        [jax.ShapeDtypeStruct(latent.shape, BF16), jax.ShapeDtypeStruct(gates.shape, F32)],
        [pltpu.VMEM((TOPK * tokens, width), F32)],
        flops=2 * total_rows * tokens * TOPK * width,
        moved=2 * back_rows * piece,
    )(returned, codes, target, gates, cotangent, apart)
    whole = pl.BlockSpec(memory_space=pltpu.VMEM)
    d_latent = call(
        latent_kernel,
        (),
        [whole, whole, whole, whole],
        whole,
        jax.ShapeDtypeStruct(latent.shape, BF16),
        flops=2 * total_rows * tokens * width,
        moved=2 * back_rows * piece,
    )(d_returned, codes, target, apart)
    return (moe_out, d_latent, gate_grad.T, grad_gate[None], grad_up[None], grad_down[None])


def solution(mesh):
    rows, blocks = P(AXES, None), P(AXES, None, None)
    return jax.shard_map(
        shards,
        mesh=mesh,
        in_specs=(rows, rows, rows, blocks, blocks, blocks, rows),
        out_specs=(rows, rows, rows, blocks, blocks, blocks),
        check_vma=False,
    )
```

```python
import functools

import jax
import jax.numpy as jnp
import numpy as np
from jax import lax
from jax.experimental import pallas as pl
from jax.experimental.pallas import tpu as pltpu
from jax.sharding import PartitionSpec as P

BF16 = jnp.bfloat16
F32 = jnp.float32
I32 = jnp.int32
TOPK = 4
CAP = 10
PIECES = 4
GROUP = 8
PLANES = 4
INNER = GROUP * CAP
SIZE = PIECES * INNER
NOTES = 16
VMEM_LIMIT = 48 * 1024 * 1024
WIDE_LIMIT = 60 * 1024 * 1024
WEIGHT = 8
SHARE_WEIGHT = 60


def dot(a, b, ca=1, cb=0):
    return lax.dot_general(a, b, (((ca,), (cb,)), ((), ())), preferred_element_type=F32)


def one_hot(mask):
    return jnp.where(mask, 1.0, 0.0).astype(BF16)


def tenth(rows):
    return (rows * 6554) >> 16


def row_numbers(count, tokens):
    return lax.broadcasted_iota(I32, (count, tokens), 0)


def slot_codes(rows, pair):
    device = tenth(rows)
    return (2 * device + pair) * CAP + rows - CAP * device


def apart_table():
    table = np.zeros((SIZE, SIZE), np.float32)
    for block in range(GROUP):
        for piece in range(PIECES):
            for slot in range(CAP):
                table[(piece * GROUP + block) * CAP + slot, (block * PIECES + piece) * CAP + slot] = 1
    return table


def call(kernel, grid, in_specs, out_specs, out_shape, scratch=(), flops=0, moved=0, limit=VMEM_LIMIT, prefetch=0, aliases=None):
    return pl.pallas_call(
        kernel,
        grid_spec=pltpu.PrefetchScalarGridSpec(
            num_scalar_prefetch=prefetch, grid=grid, in_specs=in_specs, out_specs=out_specs, scratch_shapes=list(scratch)
        ),
        out_shape=out_shape,
        input_output_aliases=aliases or {},
        compiler_params=pltpu.CompilerParams(vmem_limit_bytes=limit),
        cost_estimate=pl.CostEstimate(flops=flops, bytes_accessed=moved, transcendentals=0),
    )


def fixed(shape):
    return pl.BlockSpec(shape, lambda *i: (0,) * len(shape))


def rows_of(count, width):
    return pl.BlockSpec((count, width), lambda i, *_: (i, 0))


def in_hbm(value):
    return pltpu.with_memory_space_constraint(value, pltpu.HBM)


def column(row):
    count = row.shape[1]
    here = lax.broadcasted_iota(I32, (count, count), 0) == lax.broadcasted_iota(I32, (count, count), 1)
    return jnp.sum(jnp.where(here, row, 0), axis=1, keepdims=True)


def row_of(values):
    count = values.shape[0]
    here = lax.broadcasted_iota(I32, (count, count), 0) == lax.broadcasted_iota(I32, (count, count), 1)
    return jnp.sum(jnp.where(here, values, 0), axis=0, keepdims=True)


def pieces(rows, count=PIECES):
    width = rows.shape[1] // count
    return jnp.concatenate([rows[:, p * width : (p + 1) * width] for p in range(count)], axis=0)


def send(groups, together, sent_ref, ready, sems):
    copies = []
    for group, rows in enumerate(groups):
        ready[group] = dot(together[...], rows).astype(BF16)
        place = sent_ref.at[group * SIZE : (group + 1) * SIZE, :]
        copies.append(pltpu.make_async_copy(ready.at[group], place, sems.at[group]))
        copies[-1].start()
    for copy in copies:
        copy.wait()


def route_kernel(picks_ref, gates_ref, latent_ref, cotangent_ref, together, target_ref, shared_ref, sent_ref, notes, ready, sems):
    picks = picks_ref[...]
    tokens = picks.shape[1]
    half = sent_ref.shape[0] // 4
    names = row_numbers(2 * half // CAP, tokens)
    named = [picks[k : k + 1, :] == names for k in range(TOPK)]
    some = functools.reduce(jnp.logical_or, named)
    other = lax.broadcasted_iota(I32, (tokens, tokens), 0)
    now = lax.broadcasted_iota(I32, (tokens, tokens), 1)
    before = dot(one_hot(some), one_hot(other < now))
    slots = [jnp.sum(jnp.where(named[k], before, 0.0), axis=0, keepdims=True) for k in range(TOPK)]
    targets = [picks[k : k + 1, :] * CAP + slots[k].astype(I32) for k in range(TOPK)]
    target_ref[...] = jnp.concatenate(targets, axis=0)

    gates = [gates_ref[k : k + 1, :] for k in range(TOPK)]
    high = [g.astype(BF16).astype(F32) for g in gates]
    rest = [g - h for g, h in zip(gates, high)]
    middle = [r.astype(BF16).astype(F32) for r in rest]
    low = [r - m for r, m in zip(rest, middle)]
    values = [picks[k : k + 1, :].astype(F32) for k in range(TOPK)] + slots + high + middle + low
    across = cotangent_ref.shape[1] // tokens
    notes[...] = jnp.zeros_like(notes)
    for i, value in enumerate(values):
        notes[i // across : i // across + 1, (i % across) * tokens : (i % across + 1) * tokens] = value
    shared_ref[:tokens, :] = cotangent_ref[...]
    shared_ref[tokens:, :] = notes[...].astype(BF16)

    rows = row_numbers(half, tokens)
    parts = []
    for pair in range(2):
        codes = slot_codes(rows, pair)
        hit = functools.reduce(jnp.logical_or, [codes == target for target in targets])
        parts.append(dot(one_hot(hit), latent_ref[...]).astype(BF16))
    width = sent_ref.shape[1]
    groups = []
    for group in range(half // INNER):
        mine = slice(group * INNER, (group + 1) * INNER)
        groups.append(jnp.concatenate([part[mine, p * width : (p + 1) * width] for p in range(2) for part in parts], axis=0))
    send(groups, together, sent_ref, ready, sems)


def share_kernel(z_ref, *refs):
    shared, (together, sent_ref, ready, sems) = refs[:PLANES], refs[PLANES:]
    tokens = shared[0].shape[0] - NOTES
    across = shared[0].shape[1] // tokens
    half = sent_ref.shape[0] // PLANES
    codes = slot_codes(row_numbers(half, tokens), z_ref[0] >> 1)
    planes = []
    for plane in shared:
        notes = plane[tokens:, :].astype(F32)
        value = lambda i: notes[i // across : i // across + 1, (i % across) * tokens : (i % across + 1) * tokens]
        cotangent = plane[:tokens, :].astype(F32)
        hits, weighted = [], []
        for k in range(TOPK):
            target = (value(k) * CAP + value(TOPK + k)).astype(I32)
            gate = value(2 * TOPK + k) + value(3 * TOPK + k) + value(4 * TOPK + k)
            hits.append(one_hot(codes == target))
            weighted.append((column(gate) * cotangent).astype(BF16))
        planes.append(dot(jnp.concatenate(hits, axis=1), jnp.concatenate(weighted, axis=0)).astype(BF16))
    groups = []
    for group in range(half // INNER):
        groups.append(jnp.concatenate([rows[group * INNER : (group + 1) * INNER, :] for rows in planes], axis=0))
    send(groups, together, sent_ref, ready, sems)


def split_kernel(z_ref, moved_ref, apart, own_ref, other_ref):
    pair = z_ref[0] >> 1
    for group in range(moved_ref.shape[0] // SIZE):
        mixed = dot(apart[...], moved_ref[group * SIZE : (group + 1) * SIZE, :]).astype(BF16)
        quarters = [mixed[p * INNER : (p + 1) * INNER, :] for p in range(PIECES)]
        rows = [jnp.concatenate([quarters[i], quarters[2 + i]], axis=1) for i in range(2)]
        mine = slice(group * INNER, (group + 1) * INNER)

        @pl.when(pair == 0)
        def _():
            own_ref[mine, :] = rows[0]
            other_ref[mine, :] = rows[1]

        @pl.when(pair == 1)
        def _():
            own_ref[mine, :] = rows[1]
            other_ref[mine, :] = rows[0]


def forward_kernel(z_ref, first_ref, second_ref, w_gate, w_up, w_down, together, *refs):
    rows_ref, active_ref, slope_ref, hidden_ref, back_ref = refs[-5:]
    step = pl.program_id(0)

    @pl.when(step == 0)
    def _():
        rows_ref[0] = first_ref[...]

    @pl.when(step == 1)
    def _():
        rows_ref[0] = second_ref[...]

    rows = rows_ref[0]
    pre_gate = dot(rows, w_gate[...])
    pre_up = dot(rows, w_up[...])
    sigma = jax.nn.sigmoid(pre_gate)
    active = pre_gate * sigma
    hidden = (active * pre_up).astype(BF16)
    active_ref[0] = active
    slope_ref[0] = pre_up * (sigma * (1.0 + pre_gate * (1.0 - sigma)))
    hidden_ref[0] = hidden
    done = dot(hidden, w_down[...]).astype(BF16)
    for group in range(done.shape[0] // INNER):
        part = dot(together[...], pieces(done[group * INNER : (group + 1) * INNER, :]))
        back_ref[0, group * SIZE : (group + 1) * SIZE, :] = part.astype(BF16)


def backward_kernel(z_ref, moved_ref, active_ref, slope_ref, w_gate, w_up, w_down, apart, together, rows_ref, d_gate_ref, d_up_ref, back_ref):
    rows = dot(apart[...], moved_ref[...]).astype(BF16)
    rows_ref[...] = rows.reshape(rows_ref.shape)
    d_hidden = dot(rows, w_down[...], 1, 1)
    shape = d_hidden.shape
    d_gate = (d_hidden * slope_ref[...].reshape(shape)).astype(BF16)
    d_up = (d_hidden * active_ref[...].reshape(shape)).astype(BF16)
    d_gate_ref[...] = d_gate.reshape(d_gate_ref.shape)
    d_up_ref[...] = d_up.reshape(d_up_ref.shape)
    d_rows = (dot(d_gate, w_gate[...], 1, 1) + dot(d_up, w_up[...], 1, 1)).astype(BF16)
    for b in range(PLANES):
        part = dot(together[...], pieces(d_rows[b * INNER : (b + 1) * INNER, :]))
        back_ref[z_ref[0] ^ b, 0] = part.astype(BF16)


def unpack(back_ref, apart):
    groups = []
    for group in range(back_ref.shape[0] // SIZE):
        mixed = dot(apart[...], back_ref[group * SIZE : (group + 1) * SIZE, :]).astype(BF16)
        groups.append(jnp.concatenate([mixed[p * INNER : (p + 1) * INNER, :] for p in range(PIECES)], axis=1))
    return jnp.concatenate(groups, axis=0)


def moe_kernel(back_ref, target_ref, gates_ref, cotangent_ref, apart, moe_ref, gate_grad_ref, picked):
    step = pl.program_id(0)
    tokens = target_ref.shape[1]
    codes = slot_codes(row_numbers(back_ref.shape[0] // PIECES, tokens), step >> 1)
    hits = jnp.concatenate([one_hot(codes == target_ref[k : k + 1, :]) for k in range(TOPK)], axis=1)
    part = dot(hits, unpack(back_ref, apart), 0, 0)

    @pl.when(step == 0)
    def _():
        picked[...] = part

    @pl.when(step > 0)
    def _():
        picked[...] += part

    @pl.when(step == pl.num_programs(0) - 1)
    def _():
        cotangent = cotangent_ref[...].astype(F32)
        total = None
        for k in range(TOPK):
            mine = picked[k * tokens : (k + 1) * tokens, :]
            gate_grad_ref[k : k + 1, :] = row_of(jnp.sum(cotangent * mine, axis=1, keepdims=True))
            term = column(gates_ref[k : k + 1, :]) * mine
            total = term if total is None else total + term
        moe_ref[...] = total.astype(BF16)


def latent_kernel(back_ref, target_ref, apart, out_ref):
    tokens = target_ref.shape[1]
    half = back_ref.shape[0] // PIECES // PLANES
    hits = []
    for pair in range(2):
        codes = slot_codes(row_numbers(half, tokens), pair)
        hit = one_hot(functools.reduce(jnp.logical_or, [codes == target_ref[k : k + 1, :] for k in range(TOPK)]))
        hits += [hit, hit]
    out_ref[...] = dot(jnp.concatenate(hits, axis=0), unpack(back_ref, apart), 0, 0).astype(BF16)


def exchange(rows, blocks, axes):
    shape = rows.shape
    rows = rows.reshape(blocks, -1, shape[-1])
    return lax.all_to_all(rows, axes, split_axis=0, concat_axis=0, tiled=True).reshape(shape)


def from_plane(value, b):
    return lax.ppermute(value, "ex", [(z, z ^ b) for z in range(PLANES)])


def shards(latent, picks, gates, gate_w, up_w, down_w, cotangent):
    tokens, width = latent.shape
    columns = lax.axis_size("ep")
    devices = columns * PLANES
    w_gate, w_up, w_down = gate_w[0], up_w[0], down_w[0]
    hidden_width = w_gate.shape[1]
    plane_rows = columns * CAP
    total_rows = PLANES * plane_rows
    piece = width // PIECES
    apart, together = jnp.asarray(apart_table(), BF16), jnp.asarray(apart_table().T, BF16)
    picks, gates = picks.T, gates.T
    z = lax.axis_index("ex").astype(I32).reshape(1)
    scalar = pl.BlockSpec(memory_space=pltpu.SMEM)
    anywhere = pl.BlockSpec(memory_space=pltpu.HBM)
    whole = pl.BlockSpec(memory_space=pltpu.VMEM)
    table = fixed((SIZE, SIZE))
    groups = total_rows // SIZE

    target, shared, sent = call(
        route_kernel,
        (1,),
        [fixed(picks.shape), fixed(gates.shape), fixed(latent.shape), fixed(cotangent.shape), table],
        [fixed(picks.shape), fixed((tokens + NOTES, width)), anywhere],
        [
            jax.ShapeDtypeStruct(picks.shape, I32),
            jax.ShapeDtypeStruct((tokens + NOTES, width), BF16),
            pltpu.HBM((total_rows, width // 2), BF16),
        ],
        [
            pltpu.VMEM((NOTES, width), F32),
            pltpu.VMEM((groups, SIZE, width // 2), BF16),
            pltpu.SemaphoreType.DMA((groups,)),
        ],
        flops=2 * total_rows * tokens * width,
        moved=2 * (total_rows + tokens) * width,
    )(in_hbm(picks), in_hbm(gates), in_hbm(latent), in_hbm(cotangent), in_hbm(together))
    moved = exchange(sent, columns, "ep")
    others = [from_plane(shared, b) for b in range(1, PLANES)]
    d_sent = call(
        share_kernel,
        (),
        [scalar] + [whole] * (PLANES + 1),
        anywhere,
        pltpu.HBM((total_rows, width), BF16),
        [pltpu.VMEM((groups, SIZE, width), BF16), pltpu.SemaphoreType.DMA((groups,))],
        flops=SHARE_WEIGHT * 2 * total_rows * tokens * TOPK * width,
        moved=2 * (total_rows + tokens) * width,
    )(z, shared, *others, together)

    plane_shape = jax.ShapeDtypeStruct((plane_rows, width), BF16)
    own, other = call(
        split_kernel,
        (),
        [scalar, whole, whole],
        [whole, whole],
        [plane_shape, plane_shape],
        flops=2 * total_rows * SIZE * width,
        moved=4 * total_rows * width,
    )(z, moved, apart)
    own, other, d_sent = lax.optimization_barrier((own, other, d_sent))
    planes = [own, from_plane(own, 1), from_plane(other, 2), from_plane(other, 3)]
    d_moved = in_hbm(exchange(d_sent, columns, "ep"))

    wide = (PLANES, plane_rows, hidden_width)
    kept = [
        jax.ShapeDtypeStruct((PLANES, plane_rows, width), BF16),
        jax.ShapeDtypeStruct(wide, F32),
        jax.ShapeDtypeStruct(wide, F32),
        jax.ShapeDtypeStruct(wide, BF16),
        pltpu.HBM((PLANES, plane_rows * PIECES, piece), BF16),
    ]
    weights = [fixed(w_gate.shape), fixed(w_up.shape), fixed(w_down.shape)]
    held = ()
    for first, second in ((0, 1), (3, 2)):
        spot = lambda i, _, f=first, d=second - first: (f + d * i, 0, 0)
        turned = lambda i, z_ref, f=first, d=second - first: (z_ref[0] ^ (f + d * i), 0, 0)
        specs = [pl.BlockSpec((1,) + shape.shape[1:], spot) for shape in kept[:4]]
        specs.append(pl.BlockSpec((1,) + kept[4].shape[1:], turned))
        held = call(
            forward_kernel,
            (2,),
            [fixed((plane_rows, width))] * 2 + weights + [table] + [pl.BlockSpec(memory_space=pl.ANY)] * len(held),
            specs,
            kept,
            flops=WEIGHT * 3 * total_rows * width * hidden_width,
            moved=6 * width * hidden_width + 9 * total_rows * width,
            prefetch=1,
            aliases={7 + i: i for i in range(len(held))},
        )(z, planes[first], planes[second], w_gate, w_up, w_down, together, *held)
    rows, active, slope, hidden, back = held
    returned = in_hbm(exchange(back, devices, ("ex", "ep")).reshape(-1, piece))

    strip = lambda last: pl.BlockSpec((PLANES, INNER, last), lambda i, _: (0, i, 0))
    d_rows, d_gate, d_up, d_back = call(
        backward_kernel,
        (groups,),
        [rows_of(SIZE, width), strip(hidden_width), strip(hidden_width)] + weights + [table, table],
        [strip(width), strip(hidden_width), strip(hidden_width), pl.BlockSpec((PLANES, 1, SIZE, piece), lambda i, _: (0, i, 0, 0))],
        [
            jax.ShapeDtypeStruct((PLANES, plane_rows, width), BF16),
            jax.ShapeDtypeStruct(wide, BF16),
            jax.ShapeDtypeStruct(wide, BF16),
            pltpu.HBM((PLANES, groups, SIZE, piece), BF16),
        ],
        flops=WEIGHT * 6 * total_rows * width * hidden_width,
        moved=6 * width * hidden_width + 18 * total_rows * width,
        prefetch=1,
    )(z, d_moved, active, slope, w_gate, w_up, w_down, apart, together)
    d_returned = exchange(d_back, devices, ("ex", "ep"))

    rows, hidden, d_rows, d_gate, d_up = [v.reshape(total_rows, -1) for v in (rows, hidden, d_rows, d_gate, d_up)]
    grad_gate = jnp.dot(rows.T, d_gate, preferred_element_type=F32).astype(BF16)
    grad_up = jnp.dot(rows.T, d_up, preferred_element_type=F32).astype(BF16)
    grad_down = jnp.dot(hidden.T, d_rows, preferred_element_type=F32).astype(BF16)

    moe_out, gate_grad = call(
        moe_kernel,
        (PLANES,),
        [rows_of(plane_rows * PIECES, piece), fixed(picks.shape), fixed(gates.shape), fixed(cotangent.shape), table],
        [fixed(latent.shape), fixed(gates.shape)],
        [jax.ShapeDtypeStruct(latent.shape, BF16), jax.ShapeDtypeStruct(gates.shape, F32)],
        [pltpu.VMEM((TOPK * tokens, width), F32)],
        flops=2 * total_rows * tokens * TOPK * width,
        moved=2 * total_rows * width,
    )(returned, target, gates, cotangent, apart)
    d_latent = call(
        latent_kernel,
        (),
        [whole, whole, whole],
        whole,
        jax.ShapeDtypeStruct(latent.shape, BF16),
        flops=2 * total_rows * tokens * width,
        moved=2 * total_rows * width,
    )(d_returned.reshape(-1, piece), target, apart)
    return (moe_out, d_latent, gate_grad.T, grad_gate[None], grad_up[None], grad_down[None])


def solution(mesh):
    both = ("ep", "ex")
    rows, blocks = P(both, None), P(both, None, None)
    return jax.shard_map(
        shards,
        mesh=mesh,
        in_specs=(rows, rows, rows, blocks, blocks, blocks, rows),
        out_specs=(rows, rows, rows, blocks, blocks, blocks),
        check_vma=False,
    )
```

```python
import functools

import jax
import jax.numpy as jnp
import numpy as np
from jax import lax
from jax.experimental import pallas as pl
from jax.experimental.pallas import tpu as pltpu
from jax.sharding import PartitionSpec as P

BF16 = jnp.bfloat16
F32 = jnp.float32
I32 = jnp.int32
TOPK = 4
CAP = 10
PIECES = 4
GROUP = 4
PLANES = 4
INNER = GROUP * CAP
SIZE = PIECES * INNER
STEP_GROUP = 8
STEP_INNER = STEP_GROUP * CAP
STEP_SIZE = PIECES * STEP_INNER
NOTES = 16
VMEM_LIMIT = 48 * 1024 * 1024
WIDE_LIMIT = 60 * 1024 * 1024
WEIGHT = 8
SHARE_WEIGHT = 60


def dot(a, b, ca=1, cb=0):
    return lax.dot_general(a, b, (((ca,), (cb,)), ((), ())), preferred_element_type=F32)


def one_hot(mask):
    return jnp.where(mask, 1.0, 0.0).astype(BF16)


def tenth(rows):
    return (rows * 6554) >> 16


def row_numbers(count, tokens):
    return lax.broadcasted_iota(I32, (count, tokens), 0)


def slot_codes(rows, pair):
    device = tenth(rows)
    return (2 * device + pair) * CAP + rows - CAP * device


def apart_table(group):
    size = group * PIECES * CAP
    table = np.zeros((size, size), np.float32)
    for block in range(group):
        for piece in range(PIECES):
            for slot in range(CAP):
                table[(piece * group + block) * CAP + slot, (block * PIECES + piece) * CAP + slot] = 1
    return table


def call(kernel, grid, in_specs, out_specs, out_shape, scratch=(), flops=0, moved=0, limit=VMEM_LIMIT, prefetch=0, aliases=None):
    return pl.pallas_call(
        kernel,
        grid_spec=pltpu.PrefetchScalarGridSpec(
            num_scalar_prefetch=prefetch, grid=grid, in_specs=in_specs, out_specs=out_specs, scratch_shapes=list(scratch)
        ),
        out_shape=out_shape,
        input_output_aliases=aliases or {},
        compiler_params=pltpu.CompilerParams(vmem_limit_bytes=limit),
        cost_estimate=pl.CostEstimate(flops=flops, bytes_accessed=moved, transcendentals=0),
    )


def fixed(shape):
    return pl.BlockSpec(shape, lambda *i: (0,) * len(shape))


def rows_of(count, width):
    return pl.BlockSpec((count, width), lambda i, *_: (i, 0))


def in_hbm(value):
    return pltpu.with_memory_space_constraint(value, pltpu.HBM)


def column(row):
    count = row.shape[1]
    here = lax.broadcasted_iota(I32, (count, count), 0) == lax.broadcasted_iota(I32, (count, count), 1)
    return jnp.sum(jnp.where(here, row, 0), axis=1, keepdims=True)


def row_of(values):
    count = values.shape[0]
    here = lax.broadcasted_iota(I32, (count, count), 0) == lax.broadcasted_iota(I32, (count, count), 1)
    return jnp.sum(jnp.where(here, values, 0), axis=0, keepdims=True)


def pieces(rows, count=PIECES):
    width = rows.shape[1] // count
    return jnp.concatenate([rows[:, p * width : (p + 1) * width] for p in range(count)], axis=0)


def send(groups, together, sent_ref, ready, sems):
    copies = []
    for group, rows in enumerate(groups):
        ready[group] = dot(together[...], rows.astype(BF16)).astype(BF16)
        place = sent_ref.at[group * SIZE : (group + 1) * SIZE, :]
        copies.append(pltpu.make_async_copy(ready.at[group], place, sems.at[group]))
        copies[-1].start()
    for copy in copies:
        copy.wait()


def route_kernel(picks_ref, gates_ref, latent_ref, cotangent_ref, together, target_ref, shared_ref, sent_ref, notes, ready, sems):
    picks = picks_ref[...]
    tokens = picks.shape[1]
    half = sent_ref.shape[0] // 4
    names = row_numbers(2 * half // CAP, tokens)
    named = [picks[k : k + 1, :] == names for k in range(TOPK)]
    some = functools.reduce(jnp.logical_or, named)
    other = lax.broadcasted_iota(I32, (tokens, tokens), 0)
    now = lax.broadcasted_iota(I32, (tokens, tokens), 1)
    before = dot(one_hot(some), one_hot(other < now))
    slots = [jnp.sum(jnp.where(named[k], before, 0.0), axis=0, keepdims=True) for k in range(TOPK)]
    targets = [picks[k : k + 1, :] * CAP + slots[k].astype(I32) for k in range(TOPK)]
    target_ref[...] = jnp.concatenate(targets, axis=0)

    gates = [gates_ref[k : k + 1, :] for k in range(TOPK)]
    high = [g.astype(BF16).astype(F32) for g in gates]
    rest = [g - h for g, h in zip(gates, high)]
    middle = [r.astype(BF16).astype(F32) for r in rest]
    low = [r - m for r, m in zip(rest, middle)]
    values = [picks[k : k + 1, :].astype(F32) for k in range(TOPK)] + slots + high + middle + low
    across = cotangent_ref.shape[1] // tokens
    notes[...] = jnp.zeros_like(notes)
    for i, value in enumerate(values):
        notes[i // across : i // across + 1, (i % across) * tokens : (i % across + 1) * tokens] = value
    shared_ref[:tokens, :] = cotangent_ref[...]
    shared_ref[tokens:, :] = notes[...].astype(BF16)

    rows = row_numbers(half, tokens)
    parts = []
    for pair in range(2):
        codes = slot_codes(rows, pair)
        hit = functools.reduce(jnp.logical_or, [codes == target for target in targets])
        parts.append(dot(one_hot(hit), latent_ref[...]))
    width = sent_ref.shape[1]
    groups = []
    for group in range(half // INNER):
        mine = slice(group * INNER, (group + 1) * INNER)
        groups.append(jnp.concatenate([part[mine, p * width : (p + 1) * width] for p in range(2) for part in parts], axis=0))
    send(groups, together, sent_ref, ready, sems)


def share_kernel(z_ref, *refs):
    shared, (together, sent_ref, ready, sems) = refs[:PLANES], refs[PLANES:]
    tokens = shared[0].shape[0] - NOTES
    across = shared[0].shape[1] // tokens
    half = sent_ref.shape[0] // PLANES
    codes = slot_codes(row_numbers(half, tokens), z_ref[0] >> 1)
    planes = []
    for plane in shared:
        notes = plane[tokens:, :].astype(F32)
        value = lambda i: notes[i // across : i // across + 1, (i % across) * tokens : (i % across + 1) * tokens]
        cotangent = plane[:tokens, :].astype(F32)
        hits, weighted = [], []
        for k in range(TOPK):
            target = (value(k) * CAP + value(TOPK + k)).astype(I32)
            gate = value(2 * TOPK + k) + value(3 * TOPK + k) + value(4 * TOPK + k)
            hits.append(one_hot(codes == target))
            weighted.append((column(gate) * cotangent).astype(BF16))
        planes.append(dot(jnp.concatenate(hits, axis=1), jnp.concatenate(weighted, axis=0)))
    groups = []
    for group in range(half // INNER):
        groups.append(jnp.concatenate([rows[group * INNER : (group + 1) * INNER, :] for rows in planes], axis=0))
    send(groups, together, sent_ref, ready, sems)


def split_kernel(z_ref, moved_ref, apart, own_ref, other_ref):
    first = (z_ref[0] >> 1) == 0
    halves = [[], []]
    for group in range(moved_ref.shape[0] // SIZE):
        mixed = dot(apart[...], moved_ref[group * SIZE : (group + 1) * SIZE, :])
        for i in range(2):
            parts = [mixed[p * INNER : (p + 1) * INNER, :] for p in (i, 2 + i)]
            halves[i].append(jnp.concatenate(parts, axis=1))
    rows = [jnp.concatenate(half, axis=0) for half in halves]
    own_ref[...] = jnp.where(first, rows[0], rows[1]).astype(BF16)
    other_ref[...] = jnp.where(first, rows[1], rows[0]).astype(BF16)


def forward_kernel(z_ref, first_ref, second_ref, w_gate, w_up, w_down, together, *refs):
    rows_ref, active_ref, slope_ref, hidden_ref, back_ref = refs[-5:]
    step = pl.program_id(0)

    @pl.when(step == 0)
    def _():
        rows_ref[0] = first_ref[...]

    @pl.when(step == 1)
    def _():
        rows_ref[0] = second_ref[...]

    rows = rows_ref[0]
    pre_gate = dot(rows, w_gate[...])
    pre_up = dot(rows, w_up[...])
    sigma = jax.nn.sigmoid(pre_gate)
    active = pre_gate * sigma
    hidden = (active * pre_up).astype(BF16)
    active_ref[0] = active
    slope_ref[0] = pre_up * (sigma * (1.0 + pre_gate * (1.0 - sigma)))
    hidden_ref[0] = hidden
    done = dot(hidden, w_down[...])
    for group in range(done.shape[0] // INNER):
        part = dot(together[...], pieces(done[group * INNER : (group + 1) * INNER, :]).astype(BF16))
        back_ref[0, group * SIZE : (group + 1) * SIZE, :] = part.astype(BF16)


def backward_kernel(z_ref, moved_ref, active_ref, slope_ref, w_gate, w_up, w_down, apart, together, rows_ref, d_gate_ref, d_up_ref, back_ref):
    rows = dot(apart[...], moved_ref[...]).astype(BF16)
    rows_ref[...] = rows.reshape(rows_ref.shape)
    d_hidden = dot(rows, w_down[...], 1, 1)
    shape = d_hidden.shape
    d_gate = (d_hidden * slope_ref[...].reshape(shape)).astype(BF16)
    d_up = (d_hidden * active_ref[...].reshape(shape)).astype(BF16)
    d_gate_ref[...] = d_gate.reshape(d_gate_ref.shape)
    d_up_ref[...] = d_up.reshape(d_up_ref.shape)
    d_rows = dot(d_gate, w_gate[...], 1, 1) + dot(d_up, w_up[...], 1, 1)
    for b in range(PLANES):
        part = dot(together[...], pieces(d_rows[b * STEP_INNER : (b + 1) * STEP_INNER, :]).astype(BF16))
        back_ref[z_ref[0] ^ b, 0] = part.astype(BF16)


def unpack(back_ref, apart):
    groups = []
    for group in range(back_ref.shape[0] // SIZE):
        mixed = dot(apart[...], back_ref[group * SIZE : (group + 1) * SIZE, :])
        groups.append(jnp.concatenate([mixed[p * INNER : (p + 1) * INNER, :] for p in range(PIECES)], axis=1))
    return jnp.concatenate(groups, axis=0).astype(BF16)


def moe_kernel(back_ref, target_ref, gates_ref, cotangent_ref, apart, moe_ref, gate_grad_ref, picked):
    step = pl.program_id(0)
    tokens = target_ref.shape[1]
    codes = slot_codes(row_numbers(back_ref.shape[0] // PIECES, tokens), step >> 1)
    hits = jnp.concatenate([one_hot(codes == target_ref[k : k + 1, :]) for k in range(TOPK)], axis=1)
    part = dot(hits, unpack(back_ref, apart), 0, 0)

    @pl.when(step == 0)
    def _():
        picked[...] = part

    @pl.when(step > 0)
    def _():
        picked[...] += part

    @pl.when(step == pl.num_programs(0) - 1)
    def _():
        cotangent = cotangent_ref[...].astype(F32)
        total = None
        for k in range(TOPK):
            mine = picked[k * tokens : (k + 1) * tokens, :]
            gate_grad_ref[k : k + 1, :] = row_of(jnp.sum(cotangent * mine, axis=1, keepdims=True))
            term = column(gates_ref[k : k + 1, :]) * mine
            total = term if total is None else total + term
        moe_ref[...] = total.astype(BF16)


def latent_kernel(back_ref, target_ref, apart, out_ref):
    tokens = target_ref.shape[1]
    half = back_ref.shape[0] // PIECES // PLANES
    hits = []
    for pair in range(2):
        codes = slot_codes(row_numbers(half, tokens), pair)
        hit = one_hot(functools.reduce(jnp.logical_or, [codes == target_ref[k : k + 1, :] for k in range(TOPK)]))
        hits += [hit, hit]
    out_ref[...] = dot(jnp.concatenate(hits, axis=0), unpack(back_ref, apart), 0, 0).astype(BF16)


def exchange(rows, blocks, axes):
    shape = rows.shape
    rows = rows.reshape(blocks, -1, shape[-1])
    return lax.all_to_all(rows, axes, split_axis=0, concat_axis=0, tiled=True).reshape(shape)


def from_plane(value, b):
    return lax.ppermute(value, "ex", [(z, z ^ b) for z in range(PLANES)])


def shards(latent, picks, gates, gate_w, up_w, down_w, cotangent):
    tokens, width = latent.shape
    columns = lax.axis_size("ep")
    devices = columns * PLANES
    w_gate, w_up, w_down = gate_w[0], up_w[0], down_w[0]
    hidden_width = w_gate.shape[1]
    plane_rows = columns * CAP
    total_rows = PLANES * plane_rows
    piece = width // PIECES
    apart, together = jnp.asarray(apart_table(GROUP), BF16), jnp.asarray(apart_table(GROUP).T, BF16)
    step_apart, step_together = jnp.asarray(apart_table(STEP_GROUP), BF16), jnp.asarray(apart_table(STEP_GROUP).T, BF16)
    picks, gates = picks.T, gates.T
    z = lax.axis_index("ex").astype(I32).reshape(1)
    scalar = pl.BlockSpec(memory_space=pltpu.SMEM)
    anywhere = pl.BlockSpec(memory_space=pltpu.HBM)
    whole = pl.BlockSpec(memory_space=pltpu.VMEM)
    table = fixed((SIZE, SIZE))
    groups, steps = total_rows // SIZE, total_rows // STEP_SIZE
    step_table = fixed((STEP_SIZE, STEP_SIZE))

    target, shared, sent = call(
        route_kernel,
        (1,),
        [fixed(picks.shape), fixed(gates.shape), fixed(latent.shape), fixed(cotangent.shape), table],
        [fixed(picks.shape), fixed((tokens + NOTES, width)), anywhere],
        [
            jax.ShapeDtypeStruct(picks.shape, I32),
            jax.ShapeDtypeStruct((tokens + NOTES, width), BF16),
            pltpu.HBM((total_rows, width // 2), BF16),
        ],
        [
            pltpu.VMEM((NOTES, width), F32),
            pltpu.VMEM((groups, SIZE, width // 2), BF16),
            pltpu.SemaphoreType.DMA((groups,)),
        ],
        flops=2 * total_rows * tokens * width,
        moved=2 * (total_rows + tokens) * width,
    )(in_hbm(picks), in_hbm(gates), in_hbm(latent), in_hbm(cotangent), in_hbm(together))
    moved = exchange(sent, columns, "ep")
    others = [from_plane(shared, b) for b in range(1, PLANES)]
    d_sent = call(
        share_kernel,
        (),
        [scalar] + [whole] * (PLANES + 1),
        anywhere,
        pltpu.HBM((total_rows, width), BF16),
        [pltpu.VMEM((groups, SIZE, width), BF16), pltpu.SemaphoreType.DMA((groups,))],
        flops=SHARE_WEIGHT * 2 * total_rows * tokens * TOPK * width,
        moved=2 * (total_rows + tokens) * width,
    )(z, shared, *others, together)

    plane_shape = jax.ShapeDtypeStruct((plane_rows, width), BF16)
    own, other = call(
        split_kernel,
        (),
        [scalar, whole, whole],
        [whole, whole],
        [plane_shape, plane_shape],
        flops=2 * total_rows * SIZE * width,
        moved=4 * total_rows * width,
    )(z, moved, apart)
    own, other, d_sent = lax.optimization_barrier((own, other, d_sent))
    planes = [own, from_plane(own, 1), from_plane(other, 2), from_plane(other, 3)]
    d_moved = in_hbm(exchange(d_sent, columns, "ep"))

    wide = (PLANES, plane_rows, hidden_width)
    kept = [
        jax.ShapeDtypeStruct((PLANES, plane_rows, width), BF16),
        jax.ShapeDtypeStruct(wide, F32),
        jax.ShapeDtypeStruct(wide, F32),
        jax.ShapeDtypeStruct(wide, BF16),
        pltpu.HBM((PLANES, plane_rows * PIECES, piece), BF16),
    ]
    weights = [fixed(w_gate.shape), fixed(w_up.shape), fixed(w_down.shape)]
    held = ()
    for first, second in ((0, 1), (3, 2)):
        spot = lambda i, _, f=first, d=second - first: (f + d * i, 0, 0)
        turned = lambda i, z_ref, f=first, d=second - first: (z_ref[0] ^ (f + d * i), 0, 0)
        specs = [pl.BlockSpec((1,) + shape.shape[1:], spot) for shape in kept[:4]]
        specs.append(pl.BlockSpec((1,) + kept[4].shape[1:], turned))
        held = call(
            forward_kernel,
            (2,),
            [fixed((plane_rows, width))] * 2 + weights + [table] + [pl.BlockSpec(memory_space=pl.ANY)] * len(held),
            specs,
            kept,
            flops=WEIGHT * 3 * total_rows * width * hidden_width,
            moved=6 * width * hidden_width + 9 * total_rows * width,
            prefetch=1,
            aliases={7 + i: i for i in range(len(held))},
        )(z, planes[first], planes[second], w_gate, w_up, w_down, together, *held)
    rows, active, slope, hidden, back = held
    returned = in_hbm(exchange(back, devices, ("ex", "ep")).reshape(-1, piece))

    strip = lambda last: pl.BlockSpec((PLANES, STEP_INNER, last), lambda i, _: (0, i, 0))
    d_rows, d_gate, d_up, d_back = call(
        backward_kernel,
        (steps,),
        [rows_of(STEP_SIZE, width), strip(hidden_width), strip(hidden_width)] + weights + [step_table, step_table],
        [strip(width), strip(hidden_width), strip(hidden_width), pl.BlockSpec((PLANES, 1, STEP_SIZE, piece), lambda i, _: (0, i, 0, 0))],
        [
            jax.ShapeDtypeStruct((PLANES, plane_rows, width), BF16),
            jax.ShapeDtypeStruct(wide, BF16),
            jax.ShapeDtypeStruct(wide, BF16),
            pltpu.HBM((PLANES, steps, STEP_SIZE, piece), BF16),
        ],
        flops=WEIGHT * 6 * total_rows * width * hidden_width,
        moved=6 * width * hidden_width + 18 * total_rows * width,
        prefetch=1,
    )(z, d_moved, active, slope, w_gate, w_up, w_down, step_apart, step_together)
    d_returned = exchange(d_back, devices, ("ex", "ep"))

    rows, hidden, d_rows, d_gate, d_up = [v.reshape(total_rows, -1) for v in (rows, hidden, d_rows, d_gate, d_up)]
    grad_gate = jnp.dot(rows.T, d_gate, preferred_element_type=F32).astype(BF16)
    grad_up = jnp.dot(rows.T, d_up, preferred_element_type=F32).astype(BF16)
    grad_down = jnp.dot(hidden.T, d_rows, preferred_element_type=F32).astype(BF16)

    moe_out, gate_grad = call(
        moe_kernel,
        (PLANES,),
        [rows_of(plane_rows * PIECES, piece), fixed(picks.shape), fixed(gates.shape), fixed(cotangent.shape), table],
        [fixed(latent.shape), fixed(gates.shape)],
        [jax.ShapeDtypeStruct(latent.shape, BF16), jax.ShapeDtypeStruct(gates.shape, F32)],
        [pltpu.VMEM((TOPK * tokens, width), F32)],
        flops=2 * total_rows * tokens * TOPK * width,
        moved=2 * total_rows * width,
    )(returned, target, gates, cotangent, apart)
    d_latent = call(
        latent_kernel,
        (),
        [whole, whole, whole],
        whole,
        jax.ShapeDtypeStruct(latent.shape, BF16),
        flops=2 * total_rows * tokens * width,
        moved=2 * total_rows * width,
    )(d_returned.reshape(-1, piece), target, apart)
    return (moe_out, d_latent, gate_grad.T, grad_gate[None], grad_up[None], grad_down[None])


def solution(mesh):
    both = ("ep", "ex")
    rows, blocks = P(both, None), P(both, None, None)
    return jax.shard_map(
        shards,
        mesh=mesh,
        in_specs=(rows, rows, rows, blocks, blocks, blocks, rows),
        out_specs=(rows, rows, rows, blocks, blocks, blocks),
        check_vma=False,
    )
```

```python
import functools

import jax
import jax.numpy as jnp
import numpy as np
from jax import lax
from jax.experimental import pallas as pl
from jax.experimental.pallas import tpu as pltpu
from jax.sharding import PartitionSpec as P

BF16 = jnp.bfloat16
F32 = jnp.float32
I32 = jnp.int32
TOPK = 4
CAP = 10
PIECES = 4
GROUP = 4
PLANES = 4
INNER = GROUP * CAP
SIZE = PIECES * INNER
STEP_GROUP = 8
STEP_INNER = STEP_GROUP * CAP
STEP_SIZE = PIECES * STEP_INNER
NOTES = 16
VMEM_LIMIT = 48 * 1024 * 1024
WIDE_LIMIT = 60 * 1024 * 1024
WEIGHT = 8
SHARE_WEIGHT = 60


def dot(a, b, ca=1, cb=0):
    return lax.dot_general(a, b, (((ca,), (cb,)), ((), ())), preferred_element_type=F32)


def one_hot(mask):
    return jnp.where(mask, 1.0, 0.0).astype(BF16)


def tenth(rows):
    return (rows * 6554) >> 16


def row_numbers(count, tokens):
    return lax.broadcasted_iota(I32, (count, tokens), 0)


def slot_codes(rows, pair):
    device = tenth(rows)
    return (2 * device + pair) * CAP + rows - CAP * device


def apart_table(group):
    size = group * PIECES * CAP
    table = np.zeros((size, size), np.float32)
    for block in range(group):
        for piece in range(PIECES):
            for slot in range(CAP):
                table[(piece * group + block) * CAP + slot, (block * PIECES + piece) * CAP + slot] = 1
    return table


def call(kernel, grid, in_specs, out_specs, out_shape, scratch=(), flops=0, moved=0, limit=VMEM_LIMIT, prefetch=0, aliases=None):
    return pl.pallas_call(
        kernel,
        grid_spec=pltpu.PrefetchScalarGridSpec(
            num_scalar_prefetch=prefetch, grid=grid, in_specs=in_specs, out_specs=out_specs, scratch_shapes=list(scratch)
        ),
        out_shape=out_shape,
        input_output_aliases=aliases or {},
        compiler_params=pltpu.CompilerParams(vmem_limit_bytes=limit),
        cost_estimate=pl.CostEstimate(flops=flops, bytes_accessed=moved, transcendentals=0),
    )


def fixed(shape):
    return pl.BlockSpec(shape, lambda *i: (0,) * len(shape))


def rows_of(count, width):
    return pl.BlockSpec((count, width), lambda i, *_: (i, 0))


def in_hbm(value):
    return pltpu.with_memory_space_constraint(value, pltpu.HBM)


def column(row):
    count = row.shape[1]
    here = lax.broadcasted_iota(I32, (count, count), 0) == lax.broadcasted_iota(I32, (count, count), 1)
    return jnp.sum(jnp.where(here, row, 0), axis=1, keepdims=True)


def row_of(values):
    count = values.shape[0]
    here = lax.broadcasted_iota(I32, (count, count), 0) == lax.broadcasted_iota(I32, (count, count), 1)
    return jnp.sum(jnp.where(here, values, 0), axis=0, keepdims=True)


def pieces(rows, count=PIECES):
    width = rows.shape[1] // count
    return jnp.concatenate([rows[:, p * width : (p + 1) * width] for p in range(count)], axis=0)


def send(groups, together, sent_ref, ready, sems):
    copies = []
    for group, rows in enumerate(groups):
        ready[group] = dot(together[...], rows.astype(BF16)).astype(BF16)
        place = sent_ref.at[group * SIZE : (group + 1) * SIZE, :]
        copies.append(pltpu.make_async_copy(ready.at[group], place, sems.at[group]))
        copies[-1].start()
    for copy in copies:
        copy.wait()


def route_kernel(picks_ref, gates_ref, latent_ref, cotangent_ref, together, target_ref, shared_ref, sent_ref, notes, ready, sems):
    picks = picks_ref[...]
    tokens = picks.shape[1]
    half = sent_ref.shape[0] // 4
    names = row_numbers(2 * half // CAP, tokens)
    named = [picks[k : k + 1, :] == names for k in range(TOPK)]
    some = functools.reduce(jnp.logical_or, named)
    other = lax.broadcasted_iota(I32, (tokens, tokens), 0)
    now = lax.broadcasted_iota(I32, (tokens, tokens), 1)
    before = dot(one_hot(some), one_hot(other < now))
    slots = [jnp.sum(jnp.where(named[k], before, 0.0), axis=0, keepdims=True) for k in range(TOPK)]
    targets = [picks[k : k + 1, :] * CAP + slots[k].astype(I32) for k in range(TOPK)]
    target_ref[...] = jnp.concatenate(targets, axis=0)

    gates = [gates_ref[k : k + 1, :] for k in range(TOPK)]
    high = [g.astype(BF16).astype(F32) for g in gates]
    rest = [g - h for g, h in zip(gates, high)]
    middle = [r.astype(BF16).astype(F32) for r in rest]
    low = [r - m for r, m in zip(rest, middle)]
    values = [picks[k : k + 1, :].astype(F32) for k in range(TOPK)] + slots + high + middle + low
    across = cotangent_ref.shape[1] // tokens
    notes[...] = jnp.zeros_like(notes)
    for i, value in enumerate(values):
        notes[i // across : i // across + 1, (i % across) * tokens : (i % across + 1) * tokens] = value
    shared_ref[:tokens, :] = cotangent_ref[...]
    shared_ref[tokens:, :] = notes[...].astype(BF16)

    rows = row_numbers(half, tokens)
    parts = []
    for pair in range(2):
        codes = slot_codes(rows, pair)
        hit = functools.reduce(jnp.logical_or, [codes == target for target in targets])
        parts.append(dot(one_hot(hit), latent_ref[...]))
    width = sent_ref.shape[1]
    groups = []
    for group in range(half // INNER):
        mine = slice(group * INNER, (group + 1) * INNER)
        groups.append(jnp.concatenate([part[mine, p * width : (p + 1) * width] for p in range(2) for part in parts], axis=0))
    send(groups, together, sent_ref, ready, sems)


def share_kernel(z_ref, *refs):
    shared, (together, sent_ref, ready, sems) = refs[:PLANES], refs[PLANES:]
    tokens = shared[0].shape[0] - NOTES
    across = shared[0].shape[1] // tokens
    half = sent_ref.shape[0] // PLANES
    codes = slot_codes(row_numbers(half, tokens), z_ref[0] >> 1)
    planes = []
    for plane in shared:
        notes = plane[tokens:, :].astype(F32)
        value = lambda i: notes[i // across : i // across + 1, (i % across) * tokens : (i % across + 1) * tokens]
        cotangent = plane[:tokens, :].astype(F32)
        hits, weighted = [], []
        for k in range(TOPK):
            target = (value(k) * CAP + value(TOPK + k)).astype(I32)
            gate = value(2 * TOPK + k) + value(3 * TOPK + k) + value(4 * TOPK + k)
            hits.append(one_hot(codes == target))
            weighted.append((column(gate) * cotangent).astype(BF16))
        planes.append(dot(jnp.concatenate(hits, axis=1), jnp.concatenate(weighted, axis=0)))
    groups = []
    for group in range(half // INNER):
        groups.append(jnp.concatenate([rows[group * INNER : (group + 1) * INNER, :] for rows in planes], axis=0))
    send(groups, together, sent_ref, ready, sems)


def split_kernel(z_ref, moved_ref, apart, own_ref, other_ref):
    first = (z_ref[0] >> 1) == 0
    halves = [[], []]
    for group in range(moved_ref.shape[0] // SIZE):
        mixed = dot(apart[...], moved_ref[group * SIZE : (group + 1) * SIZE, :])
        for i in range(2):
            parts = [mixed[p * INNER : (p + 1) * INNER, :] for p in (i, 2 + i)]
            halves[i].append(jnp.concatenate(parts, axis=1))
    rows = [jnp.concatenate(half, axis=0) for half in halves]
    own_ref[...] = jnp.where(first, rows[0], rows[1]).astype(BF16)
    other_ref[...] = jnp.where(first, rows[1], rows[0]).astype(BF16)


def forward_kernel(z_ref, first_ref, second_ref, w_gate, w_up, w_down, together, *refs):
    rows_ref, active_ref, slope_ref, hidden_ref, back_ref = refs[-5:]
    step = pl.program_id(0)

    @pl.when(step == 0)
    def _():
        rows_ref[0] = first_ref[...]

    @pl.when(step == 1)
    def _():
        rows_ref[0] = second_ref[...]

    rows = rows_ref[0]
    pre_gate = dot(rows, w_gate[...])
    pre_up = dot(rows, w_up[...])
    sigma = jax.nn.sigmoid(pre_gate)
    active = pre_gate * sigma
    hidden = (active * pre_up).astype(BF16)
    active_ref[0] = active
    slope_ref[0] = pre_up * (sigma * (1.0 + pre_gate * (1.0 - sigma)))
    hidden_ref[0] = hidden
    done = dot(hidden, w_down[...])
    for group in range(done.shape[0] // INNER):
        part = dot(together[...], pieces(done[group * INNER : (group + 1) * INNER, :]).astype(BF16))
        back_ref[0, group * SIZE : (group + 1) * SIZE, :] = part.astype(BF16)


def backward_kernel(z_ref, moved_ref, active_ref, slope_ref, w_gate, w_up, w_down, apart, together, rows_ref, d_gate_ref, d_up_ref, back_ref):
    rows = dot(apart[...], moved_ref[...]).astype(BF16)
    rows_ref[...] = rows.reshape(rows_ref.shape)
    d_hidden = dot(rows, w_down[...], 1, 1)
    shape = d_hidden.shape
    d_gate = (d_hidden * slope_ref[...].reshape(shape)).astype(BF16)
    d_up = (d_hidden * active_ref[...].reshape(shape)).astype(BF16)
    d_gate_ref[...] = d_gate.reshape(d_gate_ref.shape)
    d_up_ref[...] = d_up.reshape(d_up_ref.shape)
    d_rows = dot(d_gate, w_gate[...], 1, 1) + dot(d_up, w_up[...], 1, 1)
    for b in range(PLANES):
        part = dot(together[...], pieces(d_rows[b * STEP_INNER : (b + 1) * STEP_INNER, :]).astype(BF16))
        back_ref[z_ref[0] ^ b, 0] = part.astype(BF16)


def unpack(back_ref, apart):
    groups = []
    for group in range(back_ref.shape[0] // SIZE):
        mixed = dot(apart[...], back_ref[group * SIZE : (group + 1) * SIZE, :])
        groups.append(jnp.concatenate([mixed[p * INNER : (p + 1) * INNER, :] for p in range(PIECES)], axis=1))
    return jnp.concatenate(groups, axis=0).astype(BF16)


def moe_kernel(back_ref, target_ref, gates_ref, cotangent_ref, apart, moe_ref, gate_grad_ref, picked):
    step = pl.program_id(0)
    tokens = target_ref.shape[1]
    codes = slot_codes(row_numbers(back_ref.shape[0] // PIECES, tokens), step >> 1)
    hits = jnp.concatenate([one_hot(codes == target_ref[k : k + 1, :]) for k in range(TOPK)], axis=1)
    part = dot(hits, unpack(back_ref, apart), 0, 0)

    @pl.when(step == 0)
    def _():
        picked[...] = part

    @pl.when(step > 0)
    def _():
        picked[...] += part

    @pl.when(step == pl.num_programs(0) - 1)
    def _():
        cotangent = cotangent_ref[...].astype(F32)
        total = None
        for k in range(TOPK):
            mine = picked[k * tokens : (k + 1) * tokens, :]
            gate_grad_ref[k : k + 1, :] = row_of(jnp.sum(cotangent * mine, axis=1, keepdims=True))
            term = column(gates_ref[k : k + 1, :]) * mine
            total = term if total is None else total + term
        moe_ref[...] = total.astype(BF16)


def latent_kernel(back_ref, target_ref, apart, out_ref):
    tokens = target_ref.shape[1]
    half = back_ref.shape[0] // PIECES // PLANES
    hits = []
    for pair in range(2):
        codes = slot_codes(row_numbers(half, tokens), pair)
        hit = one_hot(functools.reduce(jnp.logical_or, [codes == target_ref[k : k + 1, :] for k in range(TOPK)]))
        hits += [hit, hit]
    out_ref[...] = dot(jnp.concatenate(hits, axis=0), unpack(back_ref, apart), 0, 0).astype(BF16)


def exchange(rows, blocks, axes):
    shape = rows.shape
    rows = rows.reshape(blocks, -1, shape[-1])
    return lax.all_to_all(rows, axes, split_axis=0, concat_axis=0, tiled=True).reshape(shape)


def from_plane(value, b):
    return lax.ppermute(value, "ex", [(z, z ^ b) for z in range(PLANES)])


def shards(latent, picks, gates, gate_w, up_w, down_w, cotangent):
    tokens, width = latent.shape
    columns = lax.axis_size("ep")
    devices = columns * PLANES
    w_gate, w_up, w_down = gate_w[0], up_w[0], down_w[0]
    hidden_width = w_gate.shape[1]
    plane_rows = columns * CAP
    total_rows = PLANES * plane_rows
    piece = width // PIECES
    apart, together = jnp.asarray(apart_table(GROUP), BF16), jnp.asarray(apart_table(GROUP).T, BF16)
    step_apart, step_together = jnp.asarray(apart_table(STEP_GROUP), BF16), jnp.asarray(apart_table(STEP_GROUP).T, BF16)
    picks, gates = picks.T, gates.T
    z = lax.axis_index("ex").astype(I32).reshape(1)
    scalar = pl.BlockSpec(memory_space=pltpu.SMEM)
    anywhere = pl.BlockSpec(memory_space=pltpu.HBM)
    whole = pl.BlockSpec(memory_space=pltpu.VMEM)
    table = fixed((SIZE, SIZE))
    groups, steps = total_rows // SIZE, total_rows // STEP_SIZE
    step_table = fixed((STEP_SIZE, STEP_SIZE))

    target, shared, sent = call(
        route_kernel,
        (1,),
        [fixed(picks.shape), fixed(gates.shape), fixed(latent.shape), fixed(cotangent.shape), table],
        [fixed(picks.shape), fixed((tokens + NOTES, width)), anywhere],
        [
            jax.ShapeDtypeStruct(picks.shape, I32),
            jax.ShapeDtypeStruct((tokens + NOTES, width), BF16),
            pltpu.HBM((total_rows, width // 2), BF16),
        ],
        [
            pltpu.VMEM((NOTES, width), F32),
            pltpu.VMEM((groups, SIZE, width // 2), BF16),
            pltpu.SemaphoreType.DMA((groups,)),
        ],
        flops=2 * total_rows * tokens * width,
        moved=2 * (total_rows + tokens) * width,
    )(in_hbm(picks), in_hbm(gates), in_hbm(latent), in_hbm(cotangent), in_hbm(together))
    moved = exchange(sent, columns, "ep")
    others = [from_plane(shared, b) for b in range(1, PLANES)]
    d_sent = call(
        share_kernel,
        (),
        [scalar] + [whole] * (PLANES + 1),
        anywhere,
        pltpu.HBM((total_rows, width), BF16),
        [pltpu.VMEM((groups, SIZE, width), BF16), pltpu.SemaphoreType.DMA((groups,))],
        flops=SHARE_WEIGHT * 2 * total_rows * tokens * TOPK * width,
        moved=2 * (total_rows + tokens) * width,
    )(z, shared, *others, together)

    plane_shape = jax.ShapeDtypeStruct((plane_rows, width), BF16)
    own, other = call(
        split_kernel,
        (),
        [scalar, whole, whole],
        [whole, whole],
        [plane_shape, plane_shape],
        flops=2 * total_rows * SIZE * width,
        moved=4 * total_rows * width,
    )(z, moved, apart)
    own, other, d_sent = lax.optimization_barrier((own, other, d_sent))
    far, near, pair = from_plane(other, 2), from_plane(other, 3), from_plane(own, 1)
    planes = [own, pair, far, near]
    d_moved = in_hbm(exchange(d_sent, columns, "ep"))

    wide = (PLANES, plane_rows, hidden_width)
    kept = [
        jax.ShapeDtypeStruct((PLANES, plane_rows, width), BF16),
        jax.ShapeDtypeStruct(wide, F32),
        jax.ShapeDtypeStruct(wide, F32),
        jax.ShapeDtypeStruct(wide, BF16),
        pltpu.HBM((PLANES, plane_rows * PIECES, piece), BF16),
    ]
    weights = [fixed(w_gate.shape), fixed(w_up.shape), fixed(w_down.shape)]
    held = ()
    for first, second in ((0, 1), (3, 2)):
        spot = lambda i, _, f=first, d=second - first: (f + d * i, 0, 0)
        turned = lambda i, z_ref, f=first, d=second - first: (z_ref[0] ^ (f + d * i), 0, 0)
        specs = [pl.BlockSpec((1,) + shape.shape[1:], spot) for shape in kept[:4]]
        specs.append(pl.BlockSpec((1,) + kept[4].shape[1:], turned))
        held = call(
            forward_kernel,
            (2,),
            [fixed((plane_rows, width))] * 2 + weights + [table] + [pl.BlockSpec(memory_space=pl.ANY)] * len(held),
            specs,
            kept,
            flops=WEIGHT * 3 * total_rows * width * hidden_width,
            moved=6 * width * hidden_width + 9 * total_rows * width,
            prefetch=1,
            aliases={7 + i: i for i in range(len(held))},
        )(z, planes[first], planes[second], w_gate, w_up, w_down, together, *held)
    rows, active, slope, hidden, back = held
    returned = in_hbm(exchange(back, devices, ("ex", "ep")).reshape(-1, piece))

    strip = lambda last: pl.BlockSpec((PLANES, STEP_INNER, last), lambda i, _: (0, i, 0))
    d_rows, d_gate, d_up, d_back = call(
        backward_kernel,
        (steps,),
        [rows_of(STEP_SIZE, width), strip(hidden_width), strip(hidden_width)] + weights + [step_table, step_table],
        [strip(width), strip(hidden_width), strip(hidden_width), pl.BlockSpec((PLANES, 1, STEP_SIZE, piece), lambda i, _: (0, i, 0, 0))],
        [
            jax.ShapeDtypeStruct((PLANES, plane_rows, width), BF16),
            jax.ShapeDtypeStruct(wide, BF16),
            jax.ShapeDtypeStruct(wide, BF16),
            pltpu.HBM((PLANES, steps, STEP_SIZE, piece), BF16),
        ],
        flops=WEIGHT * 6 * total_rows * width * hidden_width,
        moved=6 * width * hidden_width + 18 * total_rows * width,
        prefetch=1,
    )(z, d_moved, active, slope, w_gate, w_up, w_down, step_apart, step_together)
    d_returned = exchange(d_back, devices, ("ex", "ep"))

    rows, hidden, d_rows, d_gate, d_up = [v.reshape(total_rows, -1) for v in (rows, hidden, d_rows, d_gate, d_up)]
    grad_gate = jnp.dot(rows.T, d_gate, preferred_element_type=F32).astype(BF16)
    grad_up = jnp.dot(rows.T, d_up, preferred_element_type=F32).astype(BF16)
    grad_down = jnp.dot(hidden.T, d_rows, preferred_element_type=F32).astype(BF16)

    moe_out, gate_grad = call(
        moe_kernel,
        (PLANES,),
        [rows_of(plane_rows * PIECES, piece), fixed(picks.shape), fixed(gates.shape), fixed(cotangent.shape), table],
        [fixed(latent.shape), fixed(gates.shape)],
        [jax.ShapeDtypeStruct(latent.shape, BF16), jax.ShapeDtypeStruct(gates.shape, F32)],
        [pltpu.VMEM((TOPK * tokens, width), F32)],
        flops=2 * total_rows * tokens * TOPK * width,
        moved=2 * total_rows * width,
    )(returned, target, gates, cotangent, apart)
    d_latent = call(
        latent_kernel,
        (),
        [whole, whole, whole],
        whole,
        jax.ShapeDtypeStruct(latent.shape, BF16),
        flops=2 * total_rows * tokens * width,
        moved=2 * total_rows * width,
    )(d_returned.reshape(-1, piece), target, apart)
    return (moe_out, d_latent, gate_grad.T, grad_gate[None], grad_up[None], grad_down[None])


def solution(mesh):
    both = ("ep", "ex")
    rows, blocks = P(both, None), P(both, None, None)
    return jax.shard_map(
        shards,
        mesh=mesh,
        in_specs=(rows, rows, rows, blocks, blocks, blocks, rows),
        out_specs=(rows, rows, rows, blocks, blocks, blocks),
        check_vma=False,
    )
```

```python
import functools

import jax
import jax.numpy as jnp
import numpy as np
from jax import lax
from jax.experimental import pallas as pl
from jax.experimental.pallas import tpu as pltpu
from jax.sharding import PartitionSpec as P

BF16 = jnp.bfloat16
F32 = jnp.float32
I32 = jnp.int32
TOPK = 4
CAP = 10
PIECES = 4
GROUP = 4
PLANES = 4
INNER = GROUP * CAP
SIZE = PIECES * INNER
STEP_GROUP = 8
STEP_INNER = STEP_GROUP * CAP
STEP_SIZE = PIECES * STEP_INNER
NOTES = 16
VMEM_LIMIT = 48 * 1024 * 1024
WIDE_LIMIT = 60 * 1024 * 1024
WEIGHT = 8
SHARE_WEIGHT = 60


def dot(a, b, ca=1, cb=0):
    return lax.dot_general(a, b, (((ca,), (cb,)), ((), ())), preferred_element_type=F32)


def one_hot(mask):
    return jnp.where(mask, 1.0, 0.0).astype(BF16)


def tenth(rows):
    return (rows * 6554) >> 16


def row_numbers(count, tokens):
    return lax.broadcasted_iota(I32, (count, tokens), 0)


def slot_codes(rows, pair):
    device = tenth(rows)
    return (2 * device + pair) * CAP + rows - CAP * device


def apart_table(group):
    size = group * PIECES * CAP
    table = np.zeros((size, size), np.float32)
    for block in range(group):
        for piece in range(PIECES):
            for slot in range(CAP):
                table[(piece * group + block) * CAP + slot, (block * PIECES + piece) * CAP + slot] = 1
    return table


def call(kernel, grid, in_specs, out_specs, out_shape, scratch=(), flops=0, moved=0, limit=VMEM_LIMIT, prefetch=0, aliases=None):
    return pl.pallas_call(
        kernel,
        grid_spec=pltpu.PrefetchScalarGridSpec(
            num_scalar_prefetch=prefetch, grid=grid, in_specs=in_specs, out_specs=out_specs, scratch_shapes=list(scratch)
        ),
        out_shape=out_shape,
        input_output_aliases=aliases or {},
        compiler_params=pltpu.CompilerParams(vmem_limit_bytes=limit),
        cost_estimate=pl.CostEstimate(flops=flops, bytes_accessed=moved, transcendentals=0),
    )


def fixed(shape):
    return pl.BlockSpec(shape, lambda *i: (0,) * len(shape))


def rows_of(count, width):
    return pl.BlockSpec((count, width), lambda i, *_: (i, 0))


def in_hbm(value):
    return pltpu.with_memory_space_constraint(value, pltpu.HBM)


def column(row):
    count = row.shape[1]
    here = lax.broadcasted_iota(I32, (count, count), 0) == lax.broadcasted_iota(I32, (count, count), 1)
    return jnp.sum(jnp.where(here, row, 0), axis=1, keepdims=True)


def row_of(values):
    count = values.shape[0]
    here = lax.broadcasted_iota(I32, (count, count), 0) == lax.broadcasted_iota(I32, (count, count), 1)
    return jnp.sum(jnp.where(here, values, 0), axis=0, keepdims=True)


def pieces(rows, count=PIECES):
    width = rows.shape[1] // count
    return jnp.concatenate([rows[:, p * width : (p + 1) * width] for p in range(count)], axis=0)


def send(groups, together, sent_ref, ready, sems):
    copies = []
    for group, rows in enumerate(groups):
        ready[group] = dot(together[...], rows.astype(BF16)).astype(BF16)
        place = sent_ref.at[group * SIZE : (group + 1) * SIZE, :]
        copies.append(pltpu.make_async_copy(ready.at[group], place, sems.at[group]))
        copies[-1].start()
    for copy in copies:
        copy.wait()


def route_kernel(picks_ref, gates_ref, latent_ref, cotangent_ref, together, target_ref, shared_ref, sent_ref, notes, ready, sems):
    picks = picks_ref[...]
    tokens = picks.shape[1]
    half = sent_ref.shape[0] // 4
    names = row_numbers(2 * half // CAP, tokens)
    named = [picks[k : k + 1, :] == names for k in range(TOPK)]
    some = functools.reduce(jnp.logical_or, named)
    other = lax.broadcasted_iota(I32, (tokens, tokens), 0)
    now = lax.broadcasted_iota(I32, (tokens, tokens), 1)
    before = dot(one_hot(some), one_hot(other < now))
    slots = [jnp.sum(jnp.where(named[k], before, 0.0), axis=0, keepdims=True) for k in range(TOPK)]
    targets = [picks[k : k + 1, :] * CAP + slots[k].astype(I32) for k in range(TOPK)]
    target_ref[...] = jnp.concatenate(targets, axis=0)

    gates = [gates_ref[k : k + 1, :] for k in range(TOPK)]
    high = [g.astype(BF16).astype(F32) for g in gates]
    rest = [g - h for g, h in zip(gates, high)]
    middle = [r.astype(BF16).astype(F32) for r in rest]
    low = [r - m for r, m in zip(rest, middle)]
    values = [picks[k : k + 1, :].astype(F32) for k in range(TOPK)] + slots + high + middle + low
    across = cotangent_ref.shape[1] // tokens
    notes[...] = jnp.zeros_like(notes)
    for i, value in enumerate(values):
        notes[i // across : i // across + 1, (i % across) * tokens : (i % across + 1) * tokens] = value
    shared_ref[:tokens, :] = cotangent_ref[...]
    shared_ref[tokens:, :] = notes[...].astype(BF16)

    rows = row_numbers(half, tokens)
    parts = []
    for pair in range(2):
        codes = slot_codes(rows, pair)
        hit = functools.reduce(jnp.logical_or, [codes == target for target in targets])
        parts.append(dot(one_hot(hit), latent_ref[...]))
    width = sent_ref.shape[1]
    groups = []
    for group in range(half // INNER):
        mine = slice(group * INNER, (group + 1) * INNER)
        groups.append(jnp.concatenate([part[mine, p * width : (p + 1) * width] for p in range(2) for part in parts], axis=0))
    send(groups, together, sent_ref, ready, sems)


def share_kernel(z_ref, *refs):
    shared, (together, sent_ref, ready, sems) = refs[:PLANES], refs[PLANES:]
    tokens = shared[0].shape[0] - NOTES
    across = shared[0].shape[1] // tokens
    half = sent_ref.shape[0] // PLANES
    codes = slot_codes(row_numbers(half, tokens), z_ref[0] >> 1)
    planes = []
    for plane in shared:
        notes = plane[tokens:, :].astype(F32)
        value = lambda i: notes[i // across : i // across + 1, (i % across) * tokens : (i % across + 1) * tokens]
        cotangent = plane[:tokens, :].astype(F32)
        hits, weighted = [], []
        for k in range(TOPK):
            target = (value(k) * CAP + value(TOPK + k)).astype(I32)
            gate = value(2 * TOPK + k) + value(3 * TOPK + k) + value(4 * TOPK + k)
            hits.append(one_hot(codes == target))
            weighted.append((column(gate) * cotangent).astype(BF16))
        planes.append(dot(jnp.concatenate(hits, axis=1), jnp.concatenate(weighted, axis=0)))
    groups = []
    for group in range(half // INNER):
        groups.append(jnp.concatenate([rows[group * INNER : (group + 1) * INNER, :] for rows in planes], axis=0))
    send(groups, together, sent_ref, ready, sems)


def split_kernel(z_ref, moved_ref, apart, own_ref, other_ref):
    first = (z_ref[0] >> 1) == 0
    halves = [[], []]
    for group in range(moved_ref.shape[0] // SIZE):
        mixed = dot(apart[...], moved_ref[group * SIZE : (group + 1) * SIZE, :])
        for i in range(2):
            parts = [mixed[p * INNER : (p + 1) * INNER, :] for p in (i, 2 + i)]
            halves[i].append(jnp.concatenate(parts, axis=1))
    rows = [jnp.concatenate(half, axis=0) for half in halves]
    own_ref[...] = jnp.where(first, rows[0], rows[1]).astype(BF16)
    other_ref[...] = jnp.where(first, rows[1], rows[0]).astype(BF16)


def forward_kernel(z_ref, first_ref, second_ref, w_gate, w_up, w_down, together, *refs):
    rows_ref, active_ref, slope_ref, hidden_ref, back_ref = refs[-5:]
    step = pl.program_id(0)

    @pl.when(step == 0)
    def _():
        rows_ref[0] = first_ref[...]

    @pl.when(step == 1)
    def _():
        rows_ref[0] = second_ref[...]

    rows = rows_ref[0]
    pre_gate = dot(rows, w_gate[...])
    pre_up = dot(rows, w_up[...])
    sigma = jax.nn.sigmoid(pre_gate)
    active = pre_gate * sigma
    hidden = (active * pre_up).astype(BF16)
    active_ref[0] = active
    slope_ref[0] = pre_up * (sigma * (1.0 + pre_gate * (1.0 - sigma)))
    hidden_ref[0] = hidden
    done = dot(hidden, w_down[...])
    for group in range(done.shape[0] // INNER):
        part = dot(together[...], pieces(done[group * INNER : (group + 1) * INNER, :]).astype(BF16))
        back_ref[0, group * SIZE : (group + 1) * SIZE, :] = part.astype(BF16)


def backward_kernel(z_ref, moved_ref, active_ref, slope_ref, w_gate, w_up, w_down, apart, together, rows_ref, d_gate_ref, d_up_ref, back_ref):
    rows = dot(apart[...], moved_ref[...]).astype(BF16)
    rows_ref[...] = rows.reshape(rows_ref.shape)
    d_hidden = dot(rows, w_down[...], 1, 1)
    shape = d_hidden.shape
    d_gate = (d_hidden * slope_ref[...].reshape(shape)).astype(BF16)
    d_up = (d_hidden * active_ref[...].reshape(shape)).astype(BF16)
    d_gate_ref[...] = d_gate.reshape(d_gate_ref.shape)
    d_up_ref[...] = d_up.reshape(d_up_ref.shape)
    d_rows = dot(d_gate, w_gate[...], 1, 1) + dot(d_up, w_up[...], 1, 1)
    for b in range(PLANES):
        part = dot(together[...], pieces(d_rows[b * STEP_INNER : (b + 1) * STEP_INNER, :]).astype(BF16))
        back_ref[z_ref[0] ^ b, 0] = part.astype(BF16)


def unpack(back_ref, apart):
    groups = []
    for group in range(back_ref.shape[0] // SIZE):
        mixed = dot(apart[...], back_ref[group * SIZE : (group + 1) * SIZE, :])
        groups.append(jnp.concatenate([mixed[p * INNER : (p + 1) * INNER, :] for p in range(PIECES)], axis=1))
    return jnp.concatenate(groups, axis=0).astype(BF16)


def moe_kernel(back_ref, target_ref, gates_ref, cotangent_ref, apart, moe_ref, gate_grad_ref, table_ref, picked, named):
    step = pl.program_id(0)
    tokens = target_ref.shape[1]
    codes = slot_codes(row_numbers(back_ref.shape[0] // PIECES, tokens), step >> 1)
    masks = [codes == target_ref[k : k + 1, :] for k in range(TOPK)]
    part = dot(jnp.concatenate([one_hot(mask) for mask in masks], axis=1), unpack(back_ref, apart), 0, 0)
    named[step] = jnp.where(functools.reduce(jnp.logical_or, masks), 1.0, 0.0)

    @pl.when(step == 0)
    def _():
        picked[...] = part

    @pl.when(step > 0)
    def _():
        picked[...] += part

    @pl.when(step == pl.num_programs(0) - 1)
    def _():
        cotangent = cotangent_ref[...].astype(F32)
        total = None
        for k in range(TOPK):
            mine = picked[k * tokens : (k + 1) * tokens, :]
            gate_grad_ref[k : k + 1, :] = row_of(jnp.sum(cotangent * mine, axis=1, keepdims=True))
            term = column(gates_ref[k : k + 1, :]) * mine
            total = term if total is None else total + term
        moe_ref[...] = total.astype(BF16)
        table_ref[...] = named[...].reshape(-1, tokens).T.astype(BF16)


def latent_kernel(back_ref, table_ref, apart, out_ref):
    out_ref[...] = dot(table_ref[...], unpack(back_ref, apart)).astype(BF16)


def exchange(rows, blocks, axes):
    shape = rows.shape
    rows = rows.reshape(blocks, -1, shape[-1])
    return lax.all_to_all(rows, axes, split_axis=0, concat_axis=0, tiled=True).reshape(shape)


def from_plane(value, b):
    return lax.ppermute(value, "ex", [(z, z ^ b) for z in range(PLANES)])


def shards(latent, picks, gates, gate_w, up_w, down_w, cotangent):
    tokens, width = latent.shape
    columns = lax.axis_size("ep")
    devices = columns * PLANES
    w_gate, w_up, w_down = gate_w[0], up_w[0], down_w[0]
    hidden_width = w_gate.shape[1]
    plane_rows = columns * CAP
    total_rows = PLANES * plane_rows
    piece = width // PIECES
    apart, together = jnp.asarray(apart_table(GROUP), BF16), jnp.asarray(apart_table(GROUP).T, BF16)
    step_apart, step_together = jnp.asarray(apart_table(STEP_GROUP), BF16), jnp.asarray(apart_table(STEP_GROUP).T, BF16)
    picks, gates = picks.T, gates.T
    z = lax.axis_index("ex").astype(I32).reshape(1)
    scalar = pl.BlockSpec(memory_space=pltpu.SMEM)
    anywhere = pl.BlockSpec(memory_space=pltpu.HBM)
    whole = pl.BlockSpec(memory_space=pltpu.VMEM)
    table = fixed((SIZE, SIZE))
    groups, steps = total_rows // SIZE, total_rows // STEP_SIZE
    step_table = fixed((STEP_SIZE, STEP_SIZE))

    target, shared, sent = call(
        route_kernel,
        (1,),
        [fixed(picks.shape), fixed(gates.shape), fixed(latent.shape), fixed(cotangent.shape), table],
        [fixed(picks.shape), fixed((tokens + NOTES, width)), anywhere],
        [
            jax.ShapeDtypeStruct(picks.shape, I32),
            jax.ShapeDtypeStruct((tokens + NOTES, width), BF16),
            pltpu.HBM((total_rows, width // 2), BF16),
        ],
        [
            pltpu.VMEM((NOTES, width), F32),
            pltpu.VMEM((groups, SIZE, width // 2), BF16),
            pltpu.SemaphoreType.DMA((groups,)),
        ],
        flops=2 * total_rows * tokens * width,
        moved=2 * (total_rows + tokens) * width,
    )(in_hbm(picks), in_hbm(gates), in_hbm(latent), in_hbm(cotangent), in_hbm(together))
    moved = exchange(sent, columns, "ep")
    others = [from_plane(shared, b) for b in range(1, PLANES)]
    d_sent = call(
        share_kernel,
        (),
        [scalar] + [whole] * (PLANES + 1),
        anywhere,
        pltpu.HBM((total_rows, width), BF16),
        [pltpu.VMEM((groups, SIZE, width), BF16), pltpu.SemaphoreType.DMA((groups,))],
        flops=SHARE_WEIGHT * 2 * total_rows * tokens * TOPK * width,
        moved=2 * (total_rows + tokens) * width,
    )(z, shared, *others, together)

    plane_shape = jax.ShapeDtypeStruct((plane_rows, width), BF16)
    own, other = call(
        split_kernel,
        (),
        [scalar, whole, whole],
        [whole, whole],
        [plane_shape, plane_shape],
        flops=2 * total_rows * SIZE * width,
        moved=4 * total_rows * width,
    )(z, moved, apart)
    own, other, d_sent = lax.optimization_barrier((own, other, d_sent))
    far, near, pair = from_plane(other, 2), from_plane(other, 3), from_plane(own, 1)
    planes = [own, pair, far, near]
    d_moved = in_hbm(exchange(d_sent, columns, "ep"))

    wide = (PLANES, plane_rows, hidden_width)
    kept = [
        jax.ShapeDtypeStruct((PLANES, plane_rows, width), BF16),
        jax.ShapeDtypeStruct(wide, F32),
        jax.ShapeDtypeStruct(wide, F32),
        jax.ShapeDtypeStruct(wide, BF16),
        pltpu.HBM((PLANES, plane_rows * PIECES, piece), BF16),
    ]
    weights = [fixed(w_gate.shape), fixed(w_up.shape), fixed(w_down.shape)]
    held = ()
    for first, second in ((0, 1), (3, 2)):
        spot = lambda i, _, f=first, d=second - first: (f + d * i, 0, 0)
        turned = lambda i, z_ref, f=first, d=second - first: (z_ref[0] ^ (f + d * i), 0, 0)
        specs = [pl.BlockSpec((1,) + shape.shape[1:], spot) for shape in kept[:4]]
        specs.append(pl.BlockSpec((1,) + kept[4].shape[1:], turned))
        held = call(
            forward_kernel,
            (2,),
            [fixed((plane_rows, width))] * 2 + weights + [table] + [pl.BlockSpec(memory_space=pl.ANY)] * len(held),
            specs,
            kept,
            flops=WEIGHT * 3 * total_rows * width * hidden_width,
            moved=6 * width * hidden_width + 9 * total_rows * width,
            prefetch=1,
            aliases={7 + i: i for i in range(len(held))},
        )(z, planes[first], planes[second], w_gate, w_up, w_down, together, *held)
    rows, active, slope, hidden, back = held
    returned = in_hbm(exchange(back, devices, ("ex", "ep")).reshape(-1, piece))

    strip = lambda last: pl.BlockSpec((PLANES, STEP_INNER, last), lambda i, _: (0, i, 0))
    d_rows, d_gate, d_up, d_back = call(
        backward_kernel,
        (steps,),
        [rows_of(STEP_SIZE, width), strip(hidden_width), strip(hidden_width)] + weights + [step_table, step_table],
        [strip(width), strip(hidden_width), strip(hidden_width), pl.BlockSpec((PLANES, 1, STEP_SIZE, piece), lambda i, _: (0, i, 0, 0))],
        [
            jax.ShapeDtypeStruct((PLANES, plane_rows, width), BF16),
            jax.ShapeDtypeStruct(wide, BF16),
            jax.ShapeDtypeStruct(wide, BF16),
            pltpu.HBM((PLANES, steps, STEP_SIZE, piece), BF16),
        ],
        flops=WEIGHT * 6 * total_rows * width * hidden_width,
        moved=6 * width * hidden_width + 18 * total_rows * width,
        prefetch=1,
    )(z, d_moved, active, slope, w_gate, w_up, w_down, step_apart, step_together)
    d_returned = exchange(d_back, devices, ("ex", "ep"))

    rows, hidden, d_rows, d_gate, d_up = [v.reshape(total_rows, -1) for v in (rows, hidden, d_rows, d_gate, d_up)]
    grad_gate = jnp.dot(rows.T, d_gate, preferred_element_type=F32).astype(BF16)
    grad_up = jnp.dot(rows.T, d_up, preferred_element_type=F32).astype(BF16)
    grad_down = jnp.dot(hidden.T, d_rows, preferred_element_type=F32).astype(BF16)

    moe_out, gate_grad, named = call(
        moe_kernel,
        (PLANES,),
        [rows_of(plane_rows * PIECES, piece), fixed(picks.shape), fixed(gates.shape), fixed(cotangent.shape), table],
        [fixed(latent.shape), fixed(gates.shape), fixed((tokens, total_rows))],
        [
            jax.ShapeDtypeStruct(latent.shape, BF16),
            jax.ShapeDtypeStruct(gates.shape, F32),
            jax.ShapeDtypeStruct((tokens, total_rows), BF16),
        ],
        [pltpu.VMEM((TOPK * tokens, width), F32), pltpu.VMEM((PLANES, plane_rows, tokens), F32)],
        flops=2 * total_rows * tokens * TOPK * width,
        moved=2 * total_rows * width,
    )(returned, target, gates, cotangent, apart)
    d_latent = call(
        latent_kernel,
        (),
        [whole, whole, whole],
        whole,
        jax.ShapeDtypeStruct(latent.shape, BF16),
        flops=2 * total_rows * tokens * width,
        moved=2 * total_rows * width,
    )(d_returned.reshape(-1, piece), named, apart)
    return (moe_out, d_latent, gate_grad.T, grad_gate[None], grad_up[None], grad_down[None])


def solution(mesh):
    both = ("ep", "ex")
    rows, blocks = P(both, None), P(both, None, None)
    return jax.shard_map(
        shards,
        mesh=mesh,
        in_specs=(rows, rows, rows, blocks, blocks, blocks, rows),
        out_specs=(rows, rows, rows, blocks, blocks, blocks),
        check_vma=False,
    )
```

```python
import functools

import jax
import jax.numpy as jnp
import numpy as np
from jax import lax
from jax.experimental import pallas as pl
from jax.experimental.pallas import tpu as pltpu
from jax.sharding import PartitionSpec as P

BF16 = jnp.bfloat16
F32 = jnp.float32
I32 = jnp.int32
TOPK = 4
CAP = 10
PIECES = 4
GROUP = 4
PLANES = 4
INNER = GROUP * CAP
SIZE = PIECES * INNER
STEP_GROUP = 8
STEP_INNER = STEP_GROUP * CAP
STEP_SIZE = PIECES * STEP_INNER
NOTES = 16
VMEM_LIMIT = 48 * 1024 * 1024
WIDE_LIMIT = 60 * 1024 * 1024
WEIGHT = 8
SHARE_WEIGHT = 60


def dot(a, b, ca=1, cb=0):
    return lax.dot_general(a, b, (((ca,), (cb,)), ((), ())), preferred_element_type=F32)


def one_hot(mask):
    return jnp.where(mask, 1.0, 0.0).astype(BF16)


def tenth(rows):
    return (rows * 6554) >> 16


def row_numbers(count, tokens):
    return lax.broadcasted_iota(I32, (count, tokens), 0)


def slot_codes(rows, pair):
    device = tenth(rows)
    return (2 * device + pair) * CAP + rows - CAP * device


def apart_table(group):
    size = group * PIECES * CAP
    table = np.zeros((size, size), np.float32)
    for block in range(group):
        for piece in range(PIECES):
            for slot in range(CAP):
                table[(piece * group + block) * CAP + slot, (block * PIECES + piece) * CAP + slot] = 1
    return table


def call(kernel, grid, in_specs, out_specs, out_shape, scratch=(), flops=0, moved=0, limit=VMEM_LIMIT, prefetch=0, aliases=None):
    return pl.pallas_call(
        kernel,
        grid_spec=pltpu.PrefetchScalarGridSpec(
            num_scalar_prefetch=prefetch, grid=grid, in_specs=in_specs, out_specs=out_specs, scratch_shapes=list(scratch)
        ),
        out_shape=out_shape,
        input_output_aliases=aliases or {},
        compiler_params=pltpu.CompilerParams(vmem_limit_bytes=limit),
        cost_estimate=pl.CostEstimate(flops=flops, bytes_accessed=moved, transcendentals=0),
    )


def fixed(shape):
    return pl.BlockSpec(shape, lambda *i: (0,) * len(shape))


def rows_of(count, width):
    return pl.BlockSpec((count, width), lambda i, *_: (i, 0))


def in_hbm(value):
    return pltpu.with_memory_space_constraint(value, pltpu.HBM)


def column(row):
    count = row.shape[1]
    here = lax.broadcasted_iota(I32, (count, count), 0) == lax.broadcasted_iota(I32, (count, count), 1)
    return jnp.sum(jnp.where(here, row, 0), axis=1, keepdims=True)


def row_of(values):
    count = values.shape[0]
    here = lax.broadcasted_iota(I32, (count, count), 0) == lax.broadcasted_iota(I32, (count, count), 1)
    return jnp.sum(jnp.where(here, values, 0), axis=0, keepdims=True)


def pieces(rows, count=PIECES):
    width = rows.shape[1] // count
    return jnp.concatenate([rows[:, p * width : (p + 1) * width] for p in range(count)], axis=0)


def send(groups, together, sent_ref, ready, sems, beside=lambda: None):
    copies = []
    for group, rows in enumerate(groups):
        ready[group] = dot(together[...], rows.astype(BF16)).astype(BF16)
        place = sent_ref.at[group * SIZE : (group + 1) * SIZE, :]
        copies.append(pltpu.make_async_copy(ready.at[group], place, sems.at[group]))
        copies[-1].start()
    beside()
    for copy in copies:
        copy.wait()


def route_kernel(picks_ref, gates_ref, latent_ref, cotangent_ref, together, target_ref, shared_ref, sent_ref, notes, ready, sems):
    picks = picks_ref[...]
    tokens = picks.shape[1]
    half = sent_ref.shape[0] // 4
    names = row_numbers(2 * half // CAP, tokens)
    named = [picks[k : k + 1, :] == names for k in range(TOPK)]
    some = functools.reduce(jnp.logical_or, named)
    other = lax.broadcasted_iota(I32, (tokens, tokens), 0)
    now = lax.broadcasted_iota(I32, (tokens, tokens), 1)
    before = dot(one_hot(some), one_hot(other < now))
    slots = [jnp.sum(jnp.where(named[k], before, 0.0), axis=0, keepdims=True) for k in range(TOPK)]
    targets = [picks[k : k + 1, :] * CAP + slots[k].astype(I32) for k in range(TOPK)]
    target_ref[...] = jnp.concatenate(targets, axis=0)

    rows = row_numbers(half, tokens)
    parts = []
    for pair in range(2):
        codes = slot_codes(rows, pair)
        hit = functools.reduce(jnp.logical_or, [codes == target for target in targets])
        parts.append(dot(one_hot(hit), latent_ref[...]))
    width = sent_ref.shape[1]
    groups = []
    for group in range(half // INNER):
        mine = slice(group * INNER, (group + 1) * INNER)
        groups.append(jnp.concatenate([part[mine, p * width : (p + 1) * width] for p in range(2) for part in parts], axis=0))
    def share():
        gates = [gates_ref[k : k + 1, :] for k in range(TOPK)]
        high = [g.astype(BF16).astype(F32) for g in gates]
        rest = [g - h for g, h in zip(gates, high)]
        middle = [r.astype(BF16).astype(F32) for r in rest]
        low = [r - m for r, m in zip(rest, middle)]
        values = [picks[k : k + 1, :].astype(F32) for k in range(TOPK)] + slots + high + middle + low
        across = cotangent_ref.shape[1] // tokens
        notes[...] = jnp.zeros_like(notes)
        for i, value in enumerate(values):
            notes[i // across : i // across + 1, (i % across) * tokens : (i % across + 1) * tokens] = value
        shared_ref[:tokens, :] = cotangent_ref[...]
        shared_ref[tokens:, :] = notes[...].astype(BF16)

    send(groups, together, sent_ref, ready, sems, share)


def share_kernel(z_ref, *refs):
    shared, (together, sent_ref, ready, sems) = refs[:PLANES], refs[PLANES:]
    tokens = shared[0].shape[0] - NOTES
    across = shared[0].shape[1] // tokens
    half = sent_ref.shape[0] // PLANES
    codes = slot_codes(row_numbers(half, tokens), z_ref[0] >> 1)
    planes = []
    for plane in shared:
        notes = plane[tokens:, :].astype(F32)
        value = lambda i: notes[i // across : i // across + 1, (i % across) * tokens : (i % across + 1) * tokens]
        cotangent = plane[:tokens, :].astype(F32)
        hits, weighted = [], []
        for k in range(TOPK):
            target = (value(k) * CAP + value(TOPK + k)).astype(I32)
            gate = value(2 * TOPK + k) + value(3 * TOPK + k) + value(4 * TOPK + k)
            hits.append(one_hot(codes == target))
            weighted.append((column(gate) * cotangent).astype(BF16))
        planes.append(dot(jnp.concatenate(hits, axis=1), jnp.concatenate(weighted, axis=0)))
    groups = []
    for group in range(half // INNER):
        groups.append(jnp.concatenate([rows[group * INNER : (group + 1) * INNER, :] for rows in planes], axis=0))
    send(groups, together, sent_ref, ready, sems)


def split_kernel(z_ref, moved_ref, apart, own_ref, other_ref):
    first = (z_ref[0] >> 1) == 0
    halves = [[], []]
    for group in range(moved_ref.shape[0] // SIZE):
        mixed = dot(apart[...], moved_ref[group * SIZE : (group + 1) * SIZE, :])
        for i in range(2):
            parts = [mixed[p * INNER : (p + 1) * INNER, :] for p in (i, 2 + i)]
            halves[i].append(jnp.concatenate(parts, axis=1))
    rows = [jnp.concatenate(half, axis=0) for half in halves]
    own_ref[...] = jnp.where(first, rows[0], rows[1]).astype(BF16)
    other_ref[...] = jnp.where(first, rows[1], rows[0]).astype(BF16)


def forward_kernel(z_ref, first_ref, second_ref, w_gate, w_up, w_down, together, *refs):
    rows_ref, active_ref, slope_ref, hidden_ref, back_ref = refs[-5:]
    step = pl.program_id(0)

    @pl.when(step == 0)
    def _():
        rows_ref[0] = first_ref[...]

    @pl.when(step == 1)
    def _():
        rows_ref[0] = second_ref[...]

    rows = rows_ref[0]
    pre_gate = dot(rows, w_gate[...])
    pre_up = dot(rows, w_up[...])
    sigma = jax.nn.sigmoid(pre_gate)
    active = pre_gate * sigma
    hidden = (active * pre_up).astype(BF16)
    active_ref[0] = active
    slope_ref[0] = pre_up * (sigma * (1.0 + pre_gate * (1.0 - sigma)))
    hidden_ref[0] = hidden
    done = dot(hidden, w_down[...])
    for group in range(done.shape[0] // INNER):
        part = dot(together[...], pieces(done[group * INNER : (group + 1) * INNER, :]).astype(BF16))
        back_ref[0, group * SIZE : (group + 1) * SIZE, :] = part.astype(BF16)


def backward_kernel(z_ref, moved_ref, active_ref, slope_ref, w_gate, w_up, w_down, apart, together, rows_ref, d_gate_ref, d_up_ref, back_ref):
    rows = dot(apart[...], moved_ref[...]).astype(BF16)
    rows_ref[...] = rows.reshape(rows_ref.shape)
    d_hidden = dot(rows, w_down[...], 1, 1)
    shape = d_hidden.shape
    d_gate = (d_hidden * slope_ref[...].reshape(shape)).astype(BF16)
    d_up = (d_hidden * active_ref[...].reshape(shape)).astype(BF16)
    d_gate_ref[...] = d_gate.reshape(d_gate_ref.shape)
    d_up_ref[...] = d_up.reshape(d_up_ref.shape)
    d_rows = dot(d_gate, w_gate[...], 1, 1) + dot(d_up, w_up[...], 1, 1)
    for b in range(PLANES):
        part = dot(together[...], pieces(d_rows[b * STEP_INNER : (b + 1) * STEP_INNER, :]).astype(BF16))
        back_ref[z_ref[0] ^ b, 0] = part.astype(BF16)


def unpack(back_ref, apart):
    groups = []
    for group in range(back_ref.shape[0] // SIZE):
        mixed = dot(apart[...], back_ref[group * SIZE : (group + 1) * SIZE, :])
        groups.append(jnp.concatenate([mixed[p * INNER : (p + 1) * INNER, :] for p in range(PIECES)], axis=1))
    return jnp.concatenate(groups, axis=0).astype(BF16)


def moe_kernel(back_ref, target_ref, gates_ref, cotangent_ref, apart, moe_ref, gate_grad_ref, table_ref, picked, named):
    step = pl.program_id(0)
    tokens = target_ref.shape[1]
    codes = slot_codes(row_numbers(back_ref.shape[0] // PIECES, tokens), step >> 1)
    masks = [codes == target_ref[k : k + 1, :] for k in range(TOPK)]
    part = dot(jnp.concatenate([one_hot(mask) for mask in masks], axis=1), unpack(back_ref, apart), 0, 0)
    named[step] = jnp.where(functools.reduce(jnp.logical_or, masks), 1.0, 0.0)

    @pl.when(step == 0)
    def _():
        picked[...] = part

    @pl.when(step > 0)
    def _():
        picked[...] += part

    @pl.when(step == pl.num_programs(0) - 1)
    def _():
        cotangent = cotangent_ref[...].astype(F32)
        total = None
        for k in range(TOPK):
            mine = picked[k * tokens : (k + 1) * tokens, :]
            gate_grad_ref[k : k + 1, :] = row_of(jnp.sum(cotangent * mine, axis=1, keepdims=True))
            term = column(gates_ref[k : k + 1, :]) * mine
            total = term if total is None else total + term
        moe_ref[...] = total.astype(BF16)
        table_ref[...] = named[...].reshape(-1, tokens).T.astype(BF16)


def latent_kernel(back_ref, table_ref, apart, out_ref):
    out_ref[...] = dot(table_ref[...], unpack(back_ref, apart)).astype(BF16)


def exchange(rows, blocks, axes):
    shape = rows.shape
    rows = rows.reshape(blocks, -1, shape[-1])
    return lax.all_to_all(rows, axes, split_axis=0, concat_axis=0, tiled=True).reshape(shape)


def from_plane(value, b):
    return lax.ppermute(value, "ex", [(z, z ^ b) for z in range(PLANES)])


def shards(latent, picks, gates, gate_w, up_w, down_w, cotangent):
    tokens, width = latent.shape
    columns = lax.axis_size("ep")
    devices = columns * PLANES
    w_gate, w_up, w_down = gate_w[0], up_w[0], down_w[0]
    hidden_width = w_gate.shape[1]
    plane_rows = columns * CAP
    total_rows = PLANES * plane_rows
    piece = width // PIECES
    apart, together = jnp.asarray(apart_table(GROUP), BF16), jnp.asarray(apart_table(GROUP).T, BF16)
    step_apart, step_together = jnp.asarray(apart_table(STEP_GROUP), BF16), jnp.asarray(apart_table(STEP_GROUP).T, BF16)
    picks, gates = picks.T, gates.T
    z = lax.axis_index("ex").astype(I32).reshape(1)
    scalar = pl.BlockSpec(memory_space=pltpu.SMEM)
    anywhere = pl.BlockSpec(memory_space=pltpu.HBM)
    whole = pl.BlockSpec(memory_space=pltpu.VMEM)
    table = fixed((SIZE, SIZE))
    groups, steps = total_rows // SIZE, total_rows // STEP_SIZE
    step_table = fixed((STEP_SIZE, STEP_SIZE))

    target, shared, sent = call(
        route_kernel,
        (1,),
        [fixed(picks.shape), fixed(gates.shape), fixed(latent.shape), fixed(cotangent.shape), table],
        [fixed(picks.shape), fixed((tokens + NOTES, width)), anywhere],
        [
            jax.ShapeDtypeStruct(picks.shape, I32),
            jax.ShapeDtypeStruct((tokens + NOTES, width), BF16),
            pltpu.HBM((total_rows, width // 2), BF16),
        ],
        [
            pltpu.VMEM((NOTES, width), F32),
            pltpu.VMEM((groups, SIZE, width // 2), BF16),
            pltpu.SemaphoreType.DMA((groups,)),
        ],
        flops=2 * total_rows * tokens * width,
        moved=2 * (total_rows + tokens) * width,
    )(in_hbm(picks), in_hbm(gates), in_hbm(latent), in_hbm(cotangent), in_hbm(together))
    moved = exchange(sent, columns, "ep")
    others = [from_plane(shared, b) for b in range(1, PLANES)]
    d_sent = call(
        share_kernel,
        (),
        [scalar] + [whole] * (PLANES + 1),
        anywhere,
        pltpu.HBM((total_rows, width), BF16),
        [pltpu.VMEM((groups, SIZE, width), BF16), pltpu.SemaphoreType.DMA((groups,))],
        flops=SHARE_WEIGHT * 2 * total_rows * tokens * TOPK * width,
        moved=2 * (total_rows + tokens) * width,
    )(z, shared, *others, together)

    plane_shape = jax.ShapeDtypeStruct((plane_rows, width), BF16)
    own, other = call(
        split_kernel,
        (),
        [scalar, whole, whole],
        [whole, whole],
        [plane_shape, plane_shape],
        flops=2 * total_rows * SIZE * width,
        moved=4 * total_rows * width,
    )(z, moved, apart)
    own, other, d_sent = lax.optimization_barrier((own, other, d_sent))
    far, near, pair = from_plane(other, 2), from_plane(other, 3), from_plane(own, 1)
    planes = [own, pair, far, near]
    d_moved = in_hbm(exchange(d_sent, columns, "ep"))

    wide = (PLANES, plane_rows, hidden_width)
    kept = [
        jax.ShapeDtypeStruct((PLANES, plane_rows, width), BF16),
        jax.ShapeDtypeStruct(wide, F32),
        jax.ShapeDtypeStruct(wide, F32),
        jax.ShapeDtypeStruct(wide, BF16),
        pltpu.HBM((PLANES, plane_rows * PIECES, piece), BF16),
    ]
    weights = [fixed(w_gate.shape), fixed(w_up.shape), fixed(w_down.shape)]
    held = ()
    for first, second in ((0, 1), (3, 2)):
        spot = lambda i, _, f=first, d=second - first: (f + d * i, 0, 0)
        turned = lambda i, z_ref, f=first, d=second - first: (z_ref[0] ^ (f + d * i), 0, 0)
        specs = [pl.BlockSpec((1,) + shape.shape[1:], spot) for shape in kept[:4]]
        specs.append(pl.BlockSpec((1,) + kept[4].shape[1:], turned))
        held = call(
            forward_kernel,
            (2,),
            [fixed((plane_rows, width))] * 2 + weights + [table] + [pl.BlockSpec(memory_space=pl.ANY)] * len(held),
            specs,
            kept,
            flops=WEIGHT * 3 * total_rows * width * hidden_width,
            moved=6 * width * hidden_width + 9 * total_rows * width,
            prefetch=1,
            aliases={7 + i: i for i in range(len(held))},
        )(z, planes[first], planes[second], w_gate, w_up, w_down, together, *held)
    rows, active, slope, hidden, back = held
    returned = in_hbm(exchange(back, devices, ("ex", "ep")).reshape(-1, piece))

    strip = lambda last: pl.BlockSpec((PLANES, STEP_INNER, last), lambda i, _: (0, i, 0))
    d_rows, d_gate, d_up, d_back = call(
        backward_kernel,
        (steps,),
        [rows_of(STEP_SIZE, width), strip(hidden_width), strip(hidden_width)] + weights + [step_table, step_table],
        [strip(width), strip(hidden_width), strip(hidden_width), pl.BlockSpec((PLANES, 1, STEP_SIZE, piece), lambda i, _: (0, i, 0, 0))],
        [
            jax.ShapeDtypeStruct((PLANES, plane_rows, width), BF16),
            jax.ShapeDtypeStruct(wide, BF16),
            jax.ShapeDtypeStruct(wide, BF16),
            pltpu.HBM((PLANES, steps, STEP_SIZE, piece), BF16),
        ],
        flops=WEIGHT * 6 * total_rows * width * hidden_width,
        moved=6 * width * hidden_width + 18 * total_rows * width,
        prefetch=1,
    )(z, d_moved, active, slope, w_gate, w_up, w_down, step_apart, step_together)
    d_returned = exchange(d_back, devices, ("ex", "ep"))

    rows, hidden, d_rows, d_gate, d_up = [v.reshape(total_rows, -1) for v in (rows, hidden, d_rows, d_gate, d_up)]
    grad_gate = jnp.dot(rows.T, d_gate, preferred_element_type=F32).astype(BF16)
    grad_up = jnp.dot(rows.T, d_up, preferred_element_type=F32).astype(BF16)
    grad_down = jnp.dot(hidden.T, d_rows, preferred_element_type=F32).astype(BF16)

    moe_out, gate_grad, named = call(
        moe_kernel,
        (PLANES,),
        [rows_of(plane_rows * PIECES, piece), fixed(picks.shape), fixed(gates.shape), fixed(cotangent.shape), table],
        [fixed(latent.shape), fixed(gates.shape), fixed((tokens, total_rows))],
        [
            jax.ShapeDtypeStruct(latent.shape, BF16),
            jax.ShapeDtypeStruct(gates.shape, F32),
            jax.ShapeDtypeStruct((tokens, total_rows), BF16),
        ],
        [pltpu.VMEM((TOPK * tokens, width), F32), pltpu.VMEM((PLANES, plane_rows, tokens), F32)],
        flops=2 * total_rows * tokens * TOPK * width,
        moved=2 * total_rows * width,
    )(returned, target, gates, cotangent, apart)
    d_latent = call(
        latent_kernel,
        (),
        [whole, whole, whole],
        whole,
        jax.ShapeDtypeStruct(latent.shape, BF16),
        flops=2 * total_rows * tokens * width,
        moved=2 * total_rows * width,
    )(d_returned.reshape(-1, piece), named, apart)
    return (moe_out, d_latent, gate_grad.T, grad_gate[None], grad_up[None], grad_down[None])


def solution(mesh):
    both = ("ep", "ex")
    rows, blocks = P(both, None), P(both, None, None)
    return jax.shard_map(
        shards,
        mesh=mesh,
        in_specs=(rows, rows, rows, blocks, blocks, blocks, rows),
        out_specs=(rows, rows, rows, blocks, blocks, blocks),
        check_vma=False,
    )
```
